256 devices in a mesh: gx: 16 (over z_lo, y), row: 8 (over z_hi, x), ta: 2 (over core).
Axes of the slice: x: 4, y: 4, z: 8 (z_hi: 2, z_lo: 4; z = z_hi * 4 + z_lo), core: 2. Of those that a mesh axis runs over, the one named last changes fastest.
Arguments:
- conserved: float32 [5, 128, 256, 256], P(None, 'gx', 'row', 'ta'), may hold values from -6 to 6
- diffusivity: float32 [5], replicated, may hold values from 0.02 to 0.1
- axial_speed: float32 [5], replicated, may hold values from 0.2 to 0.6
- coupling: float32 [5, 5], replicated, may hold values from -0.6 to 0.6
- pressure_weights: float32 [5], replicated, may hold values from 0.5 to 1.5
- station_cell: int32 [4096], P(('gx', 'row')), may hold values from 0 to 32767, as said below
- owner_row: int32 [4096, 1], P(('gx', 'row')), may hold values from 0 to 7; in each aligned block of 32 rows (0 to 31, 32 to 63, ...) at most 16 rows name the same one
- window_table: int32 [4], replicated, may hold values from 1 to 8
Outputs:
- advanced: float32 [5, 128, 256, 256], P(None, 'gx', 'row', 'ta')
- spectra: float32 [128, 128, 1056], P(('gx', 'row'), 'ta')
The draws below stay inside these ranges and needn't reach their ends.
Inputs may be any that keep to these rules, and one draw needn't show every extreme that they name: `station_cell`: entries b * 32 to (b + 1) * 32 - 1, with b = g * 8 + j, are distinct cells whose axial index lies in [g * 8, (g + 1) * 8) and radial index in [j * 32, (j + 1) * 32). `owner_row`: in each aligned block of 32 stations, no owner is named more than 16 times.
All inputs are finite; a program needn't handle non-finite values.
Results may differ from the reference program's by a relative error of at most 0.00013.
Values sent between devices are 32-bit elements; how exact they have to be, the bound alone decides.
A program may use at most 64 MiB of HBM per device.

```python
import math
import jax
import jax.numpy as jnp
import numpy as np
from jax import lax

CX = 8
CR = 32
NTH = 256
NM = 33
NFREQ = 16
STEPS = 4
STN_DEV = 32
CAP = 16
NX = 128
NR = 256
STATIONS = 4096
N_GX = 16
N_ROW = 8


def draw_station_cell(key, part):
    tiles = N_GX * N_ROW
    block_keys = jax.random.split(jax.random.fold_in(key, 11), tiles)
    chosen = jax.vmap(lambda single: jax.random.permutation(single, CX * CR)[:STN_DEV])(block_keys)
    block_index = jnp.arange(tiles, dtype=jnp.int32)
    cell_x = (block_index // N_ROW)[:, None] * CX + chosen // CR
    cell_r = (block_index % N_ROW)[:, None] * CR + chosen % CR
    return (cell_x * NR + cell_r).reshape(-1).astype(jnp.int32)


def set_ends(result, stream_key, low, top_value):
    longest = result.shape.index(max(result.shape))
    spots = []
    for shift in (0, 1):
        where = [jax.random.randint(jax.random.fold_in(stream_key, axis), (), 0, length) for axis, length in enumerate(result.shape)]
        where[longest] = (where[longest] + shift) % result.shape[longest]
        spots.append(tuple(where))
    return result.at[spots[0]].set(low).at[spots[1]].set(top_value)


def level_of(key, extent, shards, low, largest):
    factor_of = 1.0
    for dim, blocks in shards:
        draws = jax.random.uniform(jax.random.fold_in(jax.random.fold_in(key, 6), dim), (blocks,), jnp.float32, low / len(shards), largest / len(shards))
        factor_of = factor_of * jnp.repeat(jnp.exp(draws), extent[dim] // blocks).reshape((-1,) + (1,) * (len(extent) - 1 - dim))
    return factor_of


def deal_out(rng, own, number, rows, amount, top, reach, skew):
    sequence = jax.random.permutation(rng, amount)
    crowded, common = portions_of(amount, rows * top, reach, skew, True), portions_of(amount, rows * top, reach, skew, False)
    places = jnp.arange(amount)

    def named(sizes, rotation):
        used = int((sizes > 0).sum())
        fixed = max(1, used // 4)
        moved = fixed + (places - fixed + rotation * (used - fixed)) % max(1, amount - fixed)
        return jnp.zeros((amount,), jnp.int32).at[sequence[jnp.where(places < fixed, places, moved)]].set(jnp.asarray(sizes, jnp.int32))

    sizes = jnp.where(number % 4 == 0, named(crowded, number // 4), named(common, number - number // 4 - 1))
    mixed = jax.random.permutation(jax.random.fold_in(own, 3), amount)
    giver, sink = mixed[0:amount // 2 * 2:2], mixed[1:amount // 2 * 2:2]
    room = jnp.minimum(sizes[giver] - 1, reach - sizes[sink]) // 2
    room = jnp.where((giver == sequence[0]) | (sink == sequence[0]) | (sizes[sink] == 0), 0, jnp.maximum(room, 0))
    moved = jax.random.randint(jax.random.fold_in(own, 4), (amount // 2,), 0, 1 << 20) % (room + 1)
    sizes = sizes.at[giver].add(-moved).at[sink].add(moved)
    items = jnp.searchsorted(jnp.cumsum(sizes), jnp.arange(rows * top), side="right").astype(jnp.int32)
    listing = items.reshape(top, rows).T
    listing = listing[jax.random.permutation(jax.random.fold_in(own, 1), rows)]
    rotation = jax.random.randint(jax.random.fold_in(own, 2), (rows, 1), 0, top)
    return jnp.take_along_axis(listing, (jnp.arange(top)[None, :] + rotation) % top, axis=1)


def portions_of(number_of, total, limit, slope, full):
    portions = [(1 << 20) // math.isqrt(grade ** slope) + 1 for grade in range(1, number_of + 1)]
    largest = limit if full else min(limit, max(-(-total // number_of), total * portions[0] // sum(portions)))
    least = 1 if total - largest >= number_of - 1 else 0
    counts, spare = [largest] + [least] * (number_of - 1), total - largest - least * (number_of - 1)
    while spare > 0:
        movable = [i for i in range(1, number_of) if counts[i] < largest] or [i for i in range(1, number_of) if counts[i] < limit]
        mass, left = sum([portions[i] for i in movable]), spare
        for i in movable:
            extra = min(limit - counts[i], max(1, left * portions[i] // mass), spare)
            counts[i] = counts[i] + extra
            spare = spare - extra
    return np.array(counts)


def centred(stream_key, dims, deviation, bound, pieces=(), kind=jnp.bfloat16):
    drawn = jax.random.normal(stream_key, dims, jnp.float32) * deviation
    if len(pieces) > 0:
        drawn = level_of(stream_key, dims, pieces, -0.22, 0.18) * drawn
    return jnp.clip(drawn, min=-bound, max=bound).astype(kind)


def setup_inputs(seed: int = 0) -> dict:
    keys = jax.random.split(jax.random.key(seed), 9)
    conserved = centred(keys[0], (5, NX, NR, NTH), 1.0, 6.0, ((1, 16), (2, 8), (3, 2)), jnp.float32)
    diffusivity = jnp.clip(jnp.exp(jax.random.uniform(keys[1], (5,), jnp.float32, math.log(0.02), math.log(0.1))), 0.02, 0.1)
    axial_speed = jnp.clip(jax.random.uniform(keys[2], (5,), jnp.float32, 0.2, 0.6), 0.2, 0.6)
    coupling = centred(keys[3], (5, 5), 0.15, 0.6, (), jnp.float32)
    pressure_weights = jnp.clip(jax.random.uniform(keys[4], (5,), jnp.float32, 0.5, 1.5), 0.5, 1.5)
    station_cell = draw_station_cell(jax.random.fold_in(keys[8], 71), 0)
    owner_row_keys = jax.random.split(jax.random.fold_in(keys[6], 1), STATIONS // STN_DEV)
    owner_row_turns = jax.random.permutation(jax.random.fold_in(keys[6], 3), STATIONS // STN_DEV)
    owner_row = jax.vmap(lambda own, number: deal_out(jax.random.fold_in(keys[6], 2), own, number, STN_DEV, N_ROW, 1, CAP, 2))(owner_row_keys, owner_row_turns).reshape((STATIONS, 1))
    window_table = set_ends(jax.random.randint(keys[7], (STEPS,), 1, 9), jax.random.fold_in(keys[7], 1), 1, 8).astype(jnp.int32)
    return dict(conserved=conserved, diffusivity=diffusivity, axial_speed=axial_speed, coupling=coupling, pressure_weights=pressure_weights, station_cell=station_cell, owner_row=owner_row, window_table=window_table)


exact_mode = lax.Precision.HIGHEST

def change_of(padded, rate, velocity):
    lengths = (padded.shape[0] - 4, padded.shape[1] - 4, padded.shape[2] - 4)

    def shifted(offset_x, offset_r, offset_t):
        return padded[offset_x:offset_x + lengths[0], offset_r:offset_r + lengths[1], offset_t:offset_t + lengths[2]]
    center = shifted(2, 2, 2)
    near = shifted(3, 2, 2) + shifted(1, 2, 2) + shifted(2, 3, 2) + shifted(2, 1, 2) + shifted(2, 2, 3) + shifted(2, 2, 1)
    far = shifted(4, 2, 2) + shifted(0, 2, 2) + shifted(2, 4, 2) + shifted(2, 0, 2) + shifted(2, 2, 4) + shifted(2, 2, 0)
    laplace = (16.0 * near - far - 90.0 * center) / 12.0
    gradient = (8.0 * (shifted(3, 2, 2) - shifted(1, 2, 2)) - (shifted(4, 2, 2) - shifted(0, 2, 2))) / 12.0
    return rate * laplace - velocity * gradient

def azimuth_table(offset, count, total, modes):
    theta = offset + jnp.arange(count, dtype=jnp.int32)
    order = jnp.arange(modes, dtype=jnp.int32)
    turns = theta[:, None] * order[None, :] % total
    angle = 2.0 * math.pi / total * turns.astype(jnp.float32)
    return jnp.concatenate([jnp.cos(angle), jnp.sin(angle)], axis=1) * (1.0 / math.sqrt(total))

def spectral_increment(coeffs, weight, step_index, modes, freqs):
    cosine_part = coeffs[..., :modes]
    sine_part = coeffs[..., modes:]
    phase = math.pi * step_index / freqs * jnp.arange(1, freqs + 1, dtype=jnp.float32)
    cos_phase = jnp.cos(phase)[:, None]
    sin_phase = jnp.sin(phase)[:, None]
    real_part = cos_phase * cosine_part[..., None, :] - sin_phase * sine_part[..., None, :]
    imag_part = -(sin_phase * cosine_part[..., None, :] + cos_phase * sine_part[..., None, :])
    return weight * jnp.stack([real_part, imag_part], axis=-2)

def reference(conserved, diffusivity, axial_speed, coupling, pressure_weights, station_cell, owner_row, window_table):
    state = conserved
    pos_x = station_cell // NR
    pos_r = station_cell % NR
    table = azimuth_table(0, NTH, NTH, NM)
    totals = jnp.zeros((STATIONS, NFREQ, 2, NM), jnp.float32)
    for step_index in range(STEPS):
        padded = jnp.pad(state, ((0, 0), (2, 2), (2, 2), (0, 0)))
        padded = jnp.concatenate([padded[..., -2:], padded, padded[..., :2]], axis=3)
        change = lax.map(lambda item: change_of(item[0], item[1], item[2]), (padded, diffusivity, axial_speed))
        mixed = jnp.einsum('fg,gxrt->fxrt', coupling, state, precision=exact_mode)
        state = state + change + mixed
        pressure = jnp.einsum('f,fxrt->xrt', pressure_weights, state, precision=exact_mode)
        cycles = pressure[pos_x, pos_r]
        coeffs = jnp.dot(cycles, table, precision=exact_mode)
        weight = window_table[step_index].astype(jnp.float32) / 8.0
        totals = totals + spectral_increment(coeffs, weight, step_index, NM, NFREQ)
    owners = owner_row[:, 0].reshape(-1, STN_DEV)
    ordinal = jnp.arange(STN_DEV, dtype=jnp.int32)
    earlier = ordinal[None, :] < ordinal[:, None]
    same_owner = owners[:, None, :] == owners[:, :, None]
    rank = lax.optimization_barrier(jnp.sum((earlier[None] & same_owner).astype(jnp.int32), axis=2))
    block_index = jnp.arange(owners.shape[0], dtype=jnp.int32)
    row_out = (block_index // N_ROW * N_ROW)[:, None] + owners
    column = (block_index % N_ROW * CAP)[:, None] + rank
    spectra = jnp.zeros((N_GX * N_ROW, N_ROW * CAP, NFREQ * 2 * NM), jnp.float32)
    spectra = spectra.at[row_out.reshape(-1), column.reshape(-1)].add(totals.reshape(STATIONS, NFREQ * 2 * NM))
    return (state, spectra)
```

```python
import functools
import math

import jax
import jax.numpy as jnp
import numpy as np
from jax import lax
from jax.experimental import pallas as pl
from jax.experimental.pallas import tpu as pltpu
from jax.sharding import PartitionSpec as P

NF = 5
CX = 8
CR = 32
LANES = 128
NTH = 256
NM = 33
NFREQ = 16
STEPS = 4
CAP = 16
STN = 32
N_ROW = 8
SLOTS = N_ROW * CAP
COLS = NFREQ * 2 * NM
WIDE = 1152
MESH = pl.DeviceIdType.MESH
F32 = jnp.float32
BF16 = jnp.bfloat16
ORDER = (0, 3, 1, 2)
CHUNKS = 4


def split(value):
    high = value.astype(BF16)
    return high, (value - high.astype(F32)).astype(BF16)


def azimuth_tables():
    theta = np.arange(NTH)
    turns = theta[:, None] * np.arange(NM)[None, :] % NTH
    angle = 2.0 * math.pi / NTH * turns
    table = np.zeros((NTH, LANES), np.float32)
    table[:, :NM] = np.cos(angle) / math.sqrt(NTH)
    table[:, NM : 2 * NM] = np.sin(angle) / math.sqrt(NTH)
    high = table.astype(jnp.bfloat16)
    low = (table - high.astype(np.float32)).astype(jnp.bfloat16)
    high, low = high.reshape(2, LANES, LANES), low.reshape(2, LANES, LANES)
    return np.concatenate([high, high, low], axis=1)


def spread_table():
    spread = np.zeros((LANES, 2, WIDE), np.float32)
    for k in range(NFREQ):
        for part in range(2):
            for m in range(NM):
                column = (k * 2 + part) * NM + m
                spread[m, 0, column] = 1.0
                spread[NM + m, 1, column] = 1.0
    spread = spread.reshape(LANES, 2 * WIDE)
    return np.concatenate([spread, spread], axis=0).astype(jnp.bfloat16)


def phase_rows():
    rows = np.zeros((2 * STEPS, WIDE), np.float32)
    for t in range(STEPS):
        for k in range(NFREQ):
            phase = math.pi * (k + 1) * t / NFREQ
            first = slice((k * 2) * NM, (k * 2 + 1) * NM)
            second = slice((k * 2 + 1) * NM, (k * 2 + 2) * NM)
            rows[t, first] = math.cos(phase)
            rows[STEPS + t, first] = -math.sin(phase)
            rows[t, second] = -math.sin(phase)
            rows[STEPS + t, second] = -math.cos(phase)
    return rows


def kernel(
    n_gx,
    x_ref,
    diffusivity,
    axial_speed,
    coupling,
    weights,
    window,
    cell_ref,
    owner_ref,
    table_hbm,
    spread_hbm,
    phase_ref,
    out_ref,
    spectra_ref,
    s0,
    s1,
    s2,
    s3,
    mirror,
    row_out,
    row_in,
    pressure,
    place,
    table,
    spread,
    z_out,
    z_in,
    acc,
    local_sem,
    gx_send,
    gx_recv,
    ta_send,
    ta_recv,
    row_send,
    row_recv,
    z_send,
    z_recv,
):
    g, j, ta = lax.axis_index("gx"), lax.axis_index("row"), lax.axis_index("ta")
    other = 1 - ta
    state = (s0, s1, s2, s3)
    has = {("gx", 0): g > 0, ("gx", 1): g < n_gx - 1, ("row", 0): j > 0, ("row", 1): j < N_ROW - 1}
    to = {
        ("gx", 0): (g - 1, j, ta),
        ("gx", 1): (g + 1, j, ta),
        ("row", 0): (g, j - 1, ta),
        ("row", 1): (g, j + 1, ta),
    }

    loads = [
        pltpu.make_async_copy(x_ref, s0.at[:, 2 : 2 + CX, 8 : 8 + CR, :], local_sem.at[0]),
        pltpu.make_async_copy(table_hbm.at[ta], table, local_sem.at[1]),
        pltpu.make_async_copy(spread_hbm, spread, local_sem.at[2]),
    ]
    for load in loads:
        load.start()

    barrier = pltpu.get_barrier_semaphore()
    for jj in range(N_ROW):
        for tt in range(2):

            @pl.when(jnp.logical_or(j != jj, ta != tt))
            def _():
                pl.semaphore_signal(barrier, 1, device_id=(g, jj, tt), device_id_type=MESH)

    for side in range(2):

        @pl.when(has["gx", side])
        def _():
            pl.semaphore_signal(barrier, 1, device_id=to["gx", side], device_id_type=MESH)

    for side in range(2):

        @pl.when(jnp.logical_not(has["gx", side]))
        def _():
            for s in state:
                s[:, 10 * side : 10 * side + 2, 8 : 8 + CR, :] = jnp.zeros((NF, 2, CR, LANES), F32)

        @pl.when(jnp.logical_not(has["row", side]))
        def _():
            for t in range(STEPS):
                row_in[t, side] = jnp.zeros((NF, CX, 2, LANES), F32)

    for load in loads:
        load.wait()
    for f in range(NF):
        row_out[0, 0, f] = s0[f, 2 : 2 + CX, 8:10, :]
        row_out[0, 1, f] = s0[f, 2 : 2 + CX, 38:40, :]

    def gx_copy(t, side, c):
        rows = pl.ds(8 + 8 * c, 8)
        return pltpu.make_async_remote_copy(
            src_ref=state[t].at[:, pl.ds(8 * side - 2 * side + 2, 2), rows, :],
            dst_ref=state[t].at[:, pl.ds(10 - 10 * side, 2), rows, :],
            send_sem=gx_send.at[t, side, c],
            recv_sem=gx_recv.at[t, 1 - side, c],
            device_id=to["gx", side],
            device_id_type=MESH,
        )

    def gx_wait(t, side, c):
        rows = pl.ds(8 + 8 * c, 8)
        return pltpu.make_async_remote_copy(
            src_ref=state[t].at[:, pl.ds(2, 2), rows, :],
            dst_ref=state[t].at[:, pl.ds(10 * side, 2), rows, :],
            send_sem=gx_send.at[t, side, c],
            recv_sem=gx_recv.at[t, side, c],
            device_id=to["gx", side],
            device_id_type=MESH,
        )

    def row_copy(t, side):
        return pltpu.make_async_remote_copy(
            src_ref=row_out.at[t, side],
            dst_ref=row_in.at[t, 1 - side],
            send_sem=row_send.at[t, side],
            recv_sem=row_recv.at[t, 1 - side],
            device_id=to["row", side],
            device_id_type=MESH,
        )

    def row_wait(t, side):
        return pltpu.make_async_remote_copy(
            src_ref=row_out.at[t, side],
            dst_ref=row_in.at[t, side],
            send_sem=row_send.at[t, side],
            recv_sem=row_recv.at[t, side],
            device_id=to["row", side],
            device_id_type=MESH,
        )

    def ta_copy(t, c):
        return pltpu.make_async_remote_copy(
            src_ref=state[t].at[:, 2 : 2 + CX, pl.ds(8 + 8 * c, 8), :],
            dst_ref=mirror.at[t, :, :, pl.ds(8 * c, 8), :],
            send_sem=ta_send.at[t, c],
            recv_sem=ta_recv.at[t, c],
            device_id=(g, j, other),
            device_id_type=MESH,
        )

    def send_chunk(t, c):
        for side, edge in ((0, 0), (1, CHUNKS - 1)):
            if c == edge:
                pl.when(has["row", side])(row_copy(t, side).start)
        for side in range(2):
            pl.when(has["gx", side])(gx_copy(t, side, c).start)
        ta_copy(t, c).start()

    peers = 2 * N_ROW - 1 + jnp.where(g > 0, 1, 0) + jnp.where(g < n_gx - 1, 1, 0)
    pl.semaphore_wait(barrier, peers)

    for c in ORDER:
        send_chunk(0, c)

    eye = lax.broadcasted_iota(jnp.int32, (STN, STN), 0) == lax.broadcasted_iota(jnp.int32, (STN, STN), 1)
    before = lax.broadcasted_iota(jnp.int32, (STN, STN), 0) < lax.broadcasted_iota(jnp.int32, (STN, STN), 1)
    owner_across = jnp.broadcast_to(owner_ref[...], (STN, STN)).astype(F32)
    owner_down = jnp.sum(jnp.where(eye, owner_across, 0.0), axis=1, keepdims=True)
    same = jnp.logical_and(before, owner_down == owner_across)
    rank = jnp.sum(jnp.where(same, 1.0, 0.0), axis=0, keepdims=True)
    slot = owner_across[0:1] * float(CAP) + rank
    slots = lax.broadcasted_iota(jnp.int32, (SLOTS, STN), 0).astype(F32)
    slot_onehot = jnp.where(slots == slot, 1.0, 0.0).astype(BF16)
    station = cell_ref[...]
    local_cell = (station // (CR * N_ROW) - g * CX) * CR + (station % (CR * N_ROW) - j * CR)
    cell_across = jnp.broadcast_to(local_cell, (STN, STN)).astype(F32)
    cell_down = jnp.sum(jnp.where(eye, cell_across, 0.0), axis=1, keepdims=True)
    cells = lax.broadcasted_iota(jnp.int32, (STN, CX * CR), 1).astype(F32)
    cell_onehot = jnp.where(cells == cell_down, 1.0, 0.0).astype(BF16)
    place[...] = jnp.dot(slot_onehot, cell_onehot, preferred_element_type=F32).astype(BF16)

    lane = lax.broadcasted_iota(jnp.int32, (8, LANES), 1)
    first1, first2 = lane < 1, lane < 2
    last1, last2 = lane >= LANES - 1, lane >= LANES - 2
    rate = [diffusivity[f] * (1.0 / 12.0) for f in range(NF)]
    velocity = [axial_speed[f] * (1.0 / 12.0) for f in range(NF)]
    mix = [
        [coupling[f, h] + (1.0 - 7.5 * diffusivity[f] if f == h else 0.0) for h in range(NF)]
        for f in range(NF)
    ]
    press = [weights[f] for f in range(NF)]

    def step_chunk(t, c):
        s = state[t]
        r0 = 8 + 8 * c

        def body(x, carry):
            center = [s[f, x + 2, r0 : r0 + 8, :] for f in range(NF)]
            total = None
            for f in range(NF):
                v = center[f]
                o = mirror[t, f, x, 8 * c : 8 * c + 8, :]
                up1, up2 = s[f, x + 3, r0 : r0 + 8, :], s[f, x + 4, r0 : r0 + 8, :]
                dn1, dn2 = s[f, x + 1, r0 : r0 + 8, :], s[f, x, r0 : r0 + 8, :]
                near = (up1 + dn1) + (s[f, x + 2, r0 + 1 : r0 + 9, :] + s[f, x + 2, r0 - 1 : r0 + 7, :])
                far = (up2 + dn2) + (s[f, x + 2, r0 + 2 : r0 + 10, :] + s[f, x + 2, r0 - 2 : r0 + 6, :])
                near = near + (
                    pltpu.roll(jnp.where(first1, o, v), LANES - 1, 1)
                    + pltpu.roll(jnp.where(last1, o, v), 1, 1)
                )
                far = far + (
                    pltpu.roll(jnp.where(first2, o, v), LANES - 2, 1)
                    + pltpu.roll(jnp.where(last2, o, v), 2, 1)
                )
                gradient = 8.0 * (up1 - dn1) - (up2 - dn2)
                new = rate[f] * (16.0 * near - far) - velocity[f] * gradient
                for h in range(NF):
                    new = new + mix[f][h] * center[h]
                if t < STEPS - 1:
                    state[t + 1][f, x + 2, r0 : r0 + 8, :] = new
                    if c == 0:
                        row_out[t + 1, 0, f, x] = new[0:2]
                    if c == CHUNKS - 1:
                        row_out[t + 1, 1, f, x] = new[6:8]
                else:
                    out_ref[f, x, 8 * c : 8 * c + 8, :] = new
                part = press[f] * new
                total = part if total is None else total + part
            pressure[pl.ds(x * CR + 8 * c, 8), :] = total
            return carry

        lax.fori_loop(0, CX, body, 0)

    def coefficients(t):
        high, low = split(pressure[...])
        both = jnp.dot(place[...], jnp.concatenate([high, low], axis=1), preferred_element_type=F32)
        high, low = split(both[:, :LANES] + both[:, LANES:])
        z_out[t] = jnp.dot(
            jnp.concatenate([high, low, high], axis=1), table[...], preferred_element_type=F32
        ).reshape(N_ROW, CAP, LANES)

    half = j // (N_ROW // 2)
    source = (j % (N_ROW // 2)) * 2 + ta
    groups = ((0, STEPS - 1), (STEPS - 1, 1))

    def z_copy(group, owner):
        first, count = groups[group]
        return pltpu.make_async_remote_copy(
            src_ref=z_out.at[pl.ds(first, count), owner],
            dst_ref=z_in.at[source, pl.ds(first, count)],
            send_sem=z_send.at[group, owner],
            recv_sem=z_recv.at[group, source],
            device_id=(g, owner, half),
            device_id_type=MESH,
        )

    def away(owner):
        return jnp.logical_or(owner != j, half != ta)

    def z_start(group):
        for owner in range(N_ROW):
            pl.when(away(owner))(z_copy(group, owner).start)

        @pl.when(half == ta)
        def _():
            first, count = groups[group]
            for t in range(first, first + count):
                z_in[source, t] = z_out[t, j]

    def z_wait(group):
        first, count = groups[group]
        for src in range(N_ROW):
            copy = pltpu.make_async_remote_copy(
                src_ref=z_out.at[pl.ds(first, count), 0],
                dst_ref=z_in.at[src, pl.ds(first, count)],
                send_sem=z_send.at[group, 0],
                recv_sem=z_recv.at[group, src],
                device_id=(g, j, other),
                device_id_type=MESH,
            )
            mine = jnp.logical_and(half == ta, source == src)
            pl.when(jnp.logical_not(mine))(copy.wait_recv)

    def accumulate(t, start):
        w = window[t].astype(F32) * 0.125
        z = jnp.concatenate([z_in[2 * i, t] + z_in[2 * i + 1, t] for i in range(N_ROW // 2)], axis=0)
        high, low = split(z * w)
        wide = jnp.dot(jnp.concatenate([high, low], axis=1), spread[...], preferred_element_type=F32)
        new = phase_ref[t : t + 1, :] * wide[:, :WIDE] + phase_ref[STEPS + t : STEPS + t + 1, :] * wide[:, WIDE:]
        return new if start is None else start + new

    for t in range(STEPS):
        for c in ORDER:
            for side, edge in ((0, 0), (1, CHUNKS - 1)):
                if c == edge:
                    pl.when(has["row", side])(row_wait(t, side).wait_recv)
                    at = 6 if side == 0 else 8 + CR
                    for f in range(NF):
                        state[t][f, 2 : 2 + CX, at : at + 2, :] = row_in[t, side, f]
            for side in range(2):
                pl.when(has["gx", side])(gx_wait(t, side, c).wait_recv)
            ta_copy(t, c).wait_recv()
            step_chunk(t, c)
            if t < STEPS - 1:
                send_chunk(t + 1, c)
        coefficients(t)
        if t == STEPS - 2:
            z_start(0)
    z_start(1)
    z_wait(0)
    total = None
    for t in range(STEPS - 1):
        total = accumulate(t, total)
    acc[...] = total
    for t in range(STEPS):
        for c in range(CHUNKS):
            for side in range(2):
                pl.when(has["gx", side])(gx_copy(t, side, c).wait_send)
            ta_copy(t, c).wait_send()
        for side in range(2):
            pl.when(has["row", side])(row_copy(t, side).wait_send)
    for group in range(2):
        for owner in range(N_ROW):
            pl.when(away(owner))(z_copy(group, owner).wait_send)
    z_wait(1)
    spectra_ref[...] = accumulate(STEPS - 1, acc[...])[:, :COLS]


def local(n_gx, conserved, diffusivity, axial_speed, coupling, weights, station_cell, owner_row, window):
    smem = pl.BlockSpec(memory_space=pltpu.SMEM)
    vmem = pl.BlockSpec(memory_space=pltpu.VMEM)
    anywhere = pl.BlockSpec(memory_space=pl.ANY)
    big = pltpu.VMEM((NF, CX + 4, CR + 16, LANES), F32)
    dma = pltpu.SemaphoreType.DMA
    advanced, spectra = pl.pallas_call(
        functools.partial(kernel, n_gx),
        out_shape=(
            jax.ShapeDtypeStruct((NF, CX, CR, LANES), F32),
            jax.ShapeDtypeStruct((SLOTS // 2, COLS), F32),
        ),
        in_specs=[anywhere] + [smem] * 5 + [vmem] * 2 + [anywhere] * 2 + [vmem],
        out_specs=(vmem, vmem),
        scratch_shapes=[
            big,
            big,
            big,
            big,
            pltpu.VMEM((STEPS, NF, CX, CR, LANES), F32),
            pltpu.VMEM((STEPS, 2, NF, CX, 2, LANES), F32),
            pltpu.VMEM((STEPS, 2, NF, CX, 2, LANES), F32),
            pltpu.VMEM((CX * CR, LANES), F32),
            pltpu.VMEM((SLOTS, CX * CR), BF16),
            pltpu.VMEM((3 * LANES, LANES), BF16),
            pltpu.VMEM((2 * LANES, 2 * WIDE), BF16),
            pltpu.VMEM((STEPS, N_ROW, CAP, LANES), F32),
            pltpu.VMEM((N_ROW, STEPS, CAP, LANES), F32),
            pltpu.VMEM((SLOTS // 2, WIDE), F32),
            dma((3,)),
            dma((STEPS, 2, CHUNKS)),
            dma((STEPS, 2, CHUNKS)),
            dma((STEPS, CHUNKS)),
            dma((STEPS, CHUNKS)),
            dma((STEPS, 2)),
            dma((STEPS, 2)),
            dma((2, N_ROW)),
            dma((2, N_ROW)),
        ],
        compiler_params=pltpu.CompilerParams(
            collective_id=0, has_side_effects=True, vmem_limit_bytes=40 * 1024 * 1024
        ),
    )(
        conserved,
        diffusivity,
        axial_speed,
        coupling,
        weights,
        window,
        station_cell.reshape(1, STN),
        owner_row.reshape(1, STN),
        jnp.asarray(azimuth_tables()),
        jnp.asarray(spread_table()),
        jnp.asarray(phase_rows()),
    )
    return advanced, spectra[None]


def solution(mesh):
    in_specs = (
        P(None, "gx", "row", "ta"),
        P(),
        P(),
        P(),
        P(),
        P(("gx", "row")),
        P(("gx", "row"), None),
        P(),
    )
    out_specs = (P(None, "gx", "row", "ta"), P(("gx", "row"), "ta", None))
    return jax.shard_map(
        functools.partial(local, mesh.shape["gx"]),
        mesh=mesh,
        in_specs=in_specs,
        out_specs=out_specs,
        check_vma=False,
    )
```

```python
import functools
import math

import jax
import jax.numpy as jnp
import numpy as np
from jax import lax
from jax.experimental import pallas as pl
from jax.experimental.pallas import tpu as pltpu
from jax.sharding import PartitionSpec as P

NF = 5
CX = 8
CR = 32
LANES = 128
NTH = 256
NM = 33
NFREQ = 16
STEPS = 4
CAP = 16
STN = 32
N_ROW = 8
SLOTS = N_ROW * CAP
COLS = NFREQ * 2 * NM
WIDE = 1152
MESH = pl.DeviceIdType.MESH
F32 = jnp.float32
BF16 = jnp.bfloat16
ORDER = (0, 3, 1, 2)
CHUNKS = 4


def split(value):
    high = value.astype(BF16)
    return high, (value - high.astype(F32)).astype(BF16)


def azimuth_tables():
    theta = np.arange(NTH)
    turns = theta[:, None] * np.arange(NM)[None, :] % NTH
    angle = 2.0 * math.pi / NTH * turns
    table = np.zeros((NTH, LANES), np.float32)
    table[:, :NM] = np.cos(angle) / math.sqrt(NTH)
    table[:, NM : 2 * NM] = np.sin(angle) / math.sqrt(NTH)
    high = table.astype(jnp.bfloat16)
    low = (table - high.astype(np.float32)).astype(jnp.bfloat16)
    high, low = high.reshape(2, LANES, LANES), low.reshape(2, LANES, LANES)
    return np.concatenate([high, high, low], axis=1)


def spread_table():
    spread = np.zeros((LANES, 2, WIDE), np.float32)
    for k in range(NFREQ):
        for part in range(2):
            for m in range(NM):
                column = (k * 2 + part) * NM + m
                spread[m, 0, column] = 1.0
                spread[NM + m, 1, column] = 1.0
    spread = spread.reshape(LANES, 2 * WIDE)
    return np.concatenate([spread, spread], axis=0).astype(jnp.bfloat16)


def phase_rows():
    rows = np.zeros((2 * STEPS, WIDE), np.float32)
    for t in range(STEPS):
        for k in range(NFREQ):
            phase = math.pi * (k + 1) * t / NFREQ
            first = slice((k * 2) * NM, (k * 2 + 1) * NM)
            second = slice((k * 2 + 1) * NM, (k * 2 + 2) * NM)
            rows[t, first] = math.cos(phase)
            rows[STEPS + t, first] = -math.sin(phase)
            rows[t, second] = -math.sin(phase)
            rows[STEPS + t, second] = -math.cos(phase)
    return rows


def kernel(
    n_gx,
    x_ref,
    diffusivity_hbm,
    axial_speed_hbm,
    coupling_hbm,
    weights_hbm,
    window_hbm,
    cell_hbm,
    owner_hbm,
    table_hbm,
    spread_hbm,
    phase_hbm,
    out_ref,
    spectra_ref,
    s0,
    s1,
    s2,
    s3,
    mirror,
    row_out,
    row_in,
    pressure,
    place,
    table,
    spread,
    phase_ref,
    cell_ref,
    owner_ref,
    diffusivity,
    axial_speed,
    coupling,
    weights,
    window,
    z_out,
    z_in,
    acc,
    local_sem,
    gx_send,
    gx_recv,
    ta_send,
    ta_recv,
    row_send,
    row_recv,
    z_send,
    z_recv,
):
    g, j, ta = lax.axis_index("gx"), lax.axis_index("row"), lax.axis_index("ta")
    other = 1 - ta
    state = (s0, s1, s2, s3)
    has = {("gx", 0): g > 0, ("gx", 1): g < n_gx - 1, ("row", 0): j > 0, ("row", 1): j < N_ROW - 1}
    to = {
        ("gx", 0): (g - 1, j, ta),
        ("gx", 1): (g + 1, j, ta),
        ("row", 0): (g, j - 1, ta),
        ("row", 1): (g, j + 1, ta),
    }

    loads = [
        pltpu.make_async_copy(x_ref, s0.at[:, 2 : 2 + CX, 8 : 8 + CR, :], local_sem.at[0]),
        pltpu.make_async_copy(table_hbm.at[ta], table, local_sem.at[1]),
        pltpu.make_async_copy(spread_hbm, spread, local_sem.at[2]),
        pltpu.make_async_copy(phase_hbm, phase_ref, local_sem.at[3]),
        pltpu.make_async_copy(cell_hbm, cell_ref, local_sem.at[4]),
        pltpu.make_async_copy(owner_hbm, owner_ref, local_sem.at[5]),
        pltpu.make_async_copy(diffusivity_hbm, diffusivity, local_sem.at[6]),
        pltpu.make_async_copy(axial_speed_hbm, axial_speed, local_sem.at[7]),
        pltpu.make_async_copy(coupling_hbm, coupling, local_sem.at[8]),
        pltpu.make_async_copy(weights_hbm, weights, local_sem.at[9]),
        pltpu.make_async_copy(window_hbm, window, local_sem.at[10]),
    ]
    for load in loads:
        load.start()

    barrier = pltpu.get_barrier_semaphore()
    for jj in range(N_ROW):
        for tt in range(2):

            @pl.when(jnp.logical_or(j != jj, ta != tt))
            def _():
                pl.semaphore_signal(barrier, 1, device_id=(g, jj, tt), device_id_type=MESH)

    for side in range(2):

        @pl.when(has["gx", side])
        def _():
            pl.semaphore_signal(barrier, 1, device_id=to["gx", side], device_id_type=MESH)

    for side in range(2):

        @pl.when(jnp.logical_not(has["gx", side]))
        def _():
            for s in state:
                s[:, 10 * side : 10 * side + 2, 8 : 8 + CR, :] = jnp.zeros((NF, 2, CR, LANES), F32)

        @pl.when(jnp.logical_not(has["row", side]))
        def _():
            for t in range(STEPS):
                row_in[t, side] = jnp.zeros((NF, CX, 2, LANES), F32)

    loads[0].wait()
    for f in range(NF):
        row_out[0, 0, f] = s0[f, 2 : 2 + CX, 8:10, :]
        row_out[0, 1, f] = s0[f, 2 : 2 + CX, 38:40, :]

    def gx_copy(t, side, c):
        rows = pl.ds(8 + 8 * c, 8)
        return pltpu.make_async_remote_copy(
            src_ref=state[t].at[:, pl.ds(8 * side - 2 * side + 2, 2), rows, :],
            dst_ref=state[t].at[:, pl.ds(10 - 10 * side, 2), rows, :],
            send_sem=gx_send.at[t, side, c],
            recv_sem=gx_recv.at[t, 1 - side, c],
            device_id=to["gx", side],
            device_id_type=MESH,
        )

    def gx_wait(t, side, c):
        rows = pl.ds(8 + 8 * c, 8)
        return pltpu.make_async_remote_copy(
            src_ref=state[t].at[:, pl.ds(2, 2), rows, :],
            dst_ref=state[t].at[:, pl.ds(10 * side, 2), rows, :],
            send_sem=gx_send.at[t, side, c],
            recv_sem=gx_recv.at[t, side, c],
            device_id=to["gx", side],
            device_id_type=MESH,
        )

    def row_copy(t, side):
        return pltpu.make_async_remote_copy(
            src_ref=row_out.at[t, side],
            dst_ref=row_in.at[t, 1 - side],
            send_sem=row_send.at[t, side],
            recv_sem=row_recv.at[t, 1 - side],
            device_id=to["row", side],
            device_id_type=MESH,
        )

    def row_wait(t, side):
        return pltpu.make_async_remote_copy(
            src_ref=row_out.at[t, side],
            dst_ref=row_in.at[t, side],
            send_sem=row_send.at[t, side],
            recv_sem=row_recv.at[t, side],
            device_id=to["row", side],
            device_id_type=MESH,
        )

    def ta_copy(t, c):
        return pltpu.make_async_remote_copy(
            src_ref=state[t].at[:, 2 : 2 + CX, pl.ds(8 + 8 * c, 8), :],
            dst_ref=mirror.at[t, :, :, pl.ds(8 * c, 8), :],
            send_sem=ta_send.at[t, c],
            recv_sem=ta_recv.at[t, c],
            device_id=(g, j, other),
            device_id_type=MESH,
        )

    def send_chunk(t, c):
        for side, edge in ((0, 0), (1, CHUNKS - 1)):
            if c == edge:
                pl.when(has["row", side])(row_copy(t, side).start)
        for side in range(2):
            pl.when(has["gx", side])(gx_copy(t, side, c).start)
        ta_copy(t, c).start()

    peers = 2 * N_ROW - 1 + jnp.where(g > 0, 1, 0) + jnp.where(g < n_gx - 1, 1, 0)
    pl.semaphore_wait(barrier, peers)

    for c in ORDER:
        send_chunk(0, c)

    for load in loads[1:]:
        load.wait()

    eye = lax.broadcasted_iota(jnp.int32, (STN, STN), 0) == lax.broadcasted_iota(jnp.int32, (STN, STN), 1)
    before = lax.broadcasted_iota(jnp.int32, (STN, STN), 0) < lax.broadcasted_iota(jnp.int32, (STN, STN), 1)
    owner_across = jnp.broadcast_to(owner_ref[...], (STN, STN)).astype(F32)
    owner_down = jnp.sum(jnp.where(eye, owner_across, 0.0), axis=1, keepdims=True)
    same = jnp.logical_and(before, owner_down == owner_across)
    rank = jnp.sum(jnp.where(same, 1.0, 0.0), axis=0, keepdims=True)
    slot = owner_across[0:1] * float(CAP) + rank
    slots = lax.broadcasted_iota(jnp.int32, (SLOTS, STN), 0).astype(F32)
    slot_onehot = jnp.where(slots == slot, 1.0, 0.0).astype(BF16)
    station = cell_ref[...]
    local_cell = (station // (CR * N_ROW) - g * CX) * CR + (station % (CR * N_ROW) - j * CR)
    cell_across = jnp.broadcast_to(local_cell, (STN, STN)).astype(F32)
    cell_down = jnp.sum(jnp.where(eye, cell_across, 0.0), axis=1, keepdims=True)
    cells = lax.broadcasted_iota(jnp.int32, (STN, CX * CR), 1).astype(F32)
    cell_onehot = jnp.where(cells == cell_down, 1.0, 0.0).astype(BF16)
    place[...] = jnp.dot(slot_onehot, cell_onehot, preferred_element_type=F32).astype(BF16)

    lane = lax.broadcasted_iota(jnp.int32, (8, LANES), 1)
    first1, first2 = lane < 1, lane < 2
    last1, last2 = lane >= LANES - 1, lane >= LANES - 2
    rate = [diffusivity[f] * (1.0 / 12.0) for f in range(NF)]
    velocity = [axial_speed[f] * (1.0 / 12.0) for f in range(NF)]
    mix = [
        [coupling[f, h] + (1.0 - 7.5 * diffusivity[f] if f == h else 0.0) for h in range(NF)]
        for f in range(NF)
    ]
    press = [weights[f] for f in range(NF)]

    def step_chunk(t, c):
        s = state[t]
        r0 = 8 + 8 * c

        def body(x, carry):
            center = [s[f, x + 2, r0 : r0 + 8, :] for f in range(NF)]
            total = None
            for f in range(NF):
                v = center[f]
                o = mirror[t, f, x, 8 * c : 8 * c + 8, :]
                up1, up2 = s[f, x + 3, r0 : r0 + 8, :], s[f, x + 4, r0 : r0 + 8, :]
                dn1, dn2 = s[f, x + 1, r0 : r0 + 8, :], s[f, x, r0 : r0 + 8, :]
                near = (up1 + dn1) + (s[f, x + 2, r0 + 1 : r0 + 9, :] + s[f, x + 2, r0 - 1 : r0 + 7, :])
                far = (up2 + dn2) + (s[f, x + 2, r0 + 2 : r0 + 10, :] + s[f, x + 2, r0 - 2 : r0 + 6, :])
                near = near + (
                    pltpu.roll(jnp.where(first1, o, v), LANES - 1, 1)
                    + pltpu.roll(jnp.where(last1, o, v), 1, 1)
                )
                far = far + (
                    pltpu.roll(jnp.where(first2, o, v), LANES - 2, 1)
                    + pltpu.roll(jnp.where(last2, o, v), 2, 1)
                )
                gradient = 8.0 * (up1 - dn1) - (up2 - dn2)
                new = rate[f] * (16.0 * near - far) - velocity[f] * gradient
                for h in range(NF):
                    new = new + mix[f][h] * center[h]
                if t < STEPS - 1:
                    state[t + 1][f, x + 2, r0 : r0 + 8, :] = new
                    if c == 0:
                        row_out[t + 1, 0, f, x] = new[0:2]
                    if c == CHUNKS - 1:
                        row_out[t + 1, 1, f, x] = new[6:8]
                else:
                    out_ref[f, x, 8 * c : 8 * c + 8, :] = new
                part = press[f] * new
                total = part if total is None else total + part
            pressure[pl.ds(x * CR + 8 * c, 8), :] = total
            return carry

        lax.fori_loop(0, CX, body, 0, unroll=True)

    def coefficients(t):
        high, low = split(pressure[...])
        both = jnp.dot(place[...], jnp.concatenate([high, low], axis=1), preferred_element_type=F32)
        high, low = split(both[:, :LANES] + both[:, LANES:])
        z_out[t] = jnp.dot(
            jnp.concatenate([high, low, high], axis=1), table[...], preferred_element_type=F32
        ).reshape(N_ROW, CAP, LANES)

    half = j // (N_ROW // 2)
    source = (j % (N_ROW // 2)) * 2 + ta
    groups = ((0, STEPS - 1), (STEPS - 1, 1))

    def z_copy(group, owner):
        first, count = groups[group]
        return pltpu.make_async_remote_copy(
            src_ref=z_out.at[pl.ds(first, count), owner],
            dst_ref=z_in.at[source, pl.ds(first, count)],
            send_sem=z_send.at[group, owner],
            recv_sem=z_recv.at[group, source],
            device_id=(g, owner, half),
            device_id_type=MESH,
        )

    def away(owner):
        return jnp.logical_or(owner != j, half != ta)

    def z_start(group):
        for owner in range(N_ROW):
            pl.when(away(owner))(z_copy(group, owner).start)

        @pl.when(half == ta)
        def _():
            first, count = groups[group]
            for t in range(first, first + count):
                z_in[source, t] = z_out[t, j]

    def z_wait(group):
        first, count = groups[group]
        for src in range(N_ROW):
            copy = pltpu.make_async_remote_copy(
                src_ref=z_out.at[pl.ds(first, count), 0],
                dst_ref=z_in.at[src, pl.ds(first, count)],
                send_sem=z_send.at[group, 0],
                recv_sem=z_recv.at[group, src],
                device_id=(g, j, other),
                device_id_type=MESH,
            )
            mine = jnp.logical_and(half == ta, source == src)
            pl.when(jnp.logical_not(mine))(copy.wait_recv)

    def accumulate(t, start):
        w = window[t].astype(F32) * 0.125
        z = jnp.concatenate([z_in[2 * i, t] + z_in[2 * i + 1, t] for i in range(N_ROW // 2)], axis=0)
        high, low = split(z * w)
        wide = jnp.dot(jnp.concatenate([high, low], axis=1), spread[...], preferred_element_type=F32)
        new = phase_ref[t : t + 1, :] * wide[:, :WIDE] + phase_ref[STEPS + t : STEPS + t + 1, :] * wide[:, WIDE:]
        return new if start is None else start + new

    for t in range(STEPS):
        for c in ORDER:
            for side, edge in ((0, 0), (1, CHUNKS - 1)):
                if c == edge:
                    pl.when(has["row", side])(row_wait(t, side).wait_recv)
                    at = 6 if side == 0 else 8 + CR
                    for f in range(NF):
                        state[t][f, 2 : 2 + CX, at : at + 2, :] = row_in[t, side, f]
            for side in range(2):
                pl.when(has["gx", side])(gx_wait(t, side, c).wait_recv)
            ta_copy(t, c).wait_recv()
            step_chunk(t, c)
            if t < STEPS - 1:
                send_chunk(t + 1, c)
        coefficients(t)
        if t == STEPS - 2:
            z_start(0)
    z_start(1)
    z_wait(0)
    total = None
    for t in range(STEPS - 1):
        total = accumulate(t, total)
    acc[...] = total
    for t in range(STEPS):
        for c in range(CHUNKS):
            for side in range(2):
                pl.when(has["gx", side])(gx_copy(t, side, c).wait_send)
            ta_copy(t, c).wait_send()
        for side in range(2):
            pl.when(has["row", side])(row_copy(t, side).wait_send)
    for group in range(2):
        for owner in range(N_ROW):
            pl.when(away(owner))(z_copy(group, owner).wait_send)
    z_wait(1)
    spectra_ref[...] = accumulate(STEPS - 1, acc[...])[:, :COLS]


def local(n_gx, conserved, diffusivity, axial_speed, coupling, weights, station_cell, owner_row, window):
    vmem = pl.BlockSpec(memory_space=pltpu.VMEM)
    hbm = pl.BlockSpec(memory_space=pltpu.HBM)
    big = pltpu.VMEM((NF, CX + 4, CR + 16, LANES), F32)
    dma = pltpu.SemaphoreType.DMA
    advanced, spectra = pl.pallas_call(
        functools.partial(kernel, n_gx),
        out_shape=(
            jax.ShapeDtypeStruct((NF, CX, CR, LANES), F32),
            jax.ShapeDtypeStruct((SLOTS // 2, COLS), F32),
        ),
        in_specs=[hbm] * 11,
        out_specs=(vmem, vmem),
        scratch_shapes=[
            big,
            big,
            big,
            big,
            pltpu.VMEM((STEPS, NF, CX, CR, LANES), F32),
            pltpu.VMEM((STEPS, 2, NF, CX, 2, LANES), F32),
            pltpu.VMEM((STEPS, 2, NF, CX, 2, LANES), F32),
            pltpu.VMEM((CX * CR, LANES), F32),
            pltpu.VMEM((SLOTS, CX * CR), BF16),
            pltpu.VMEM((3 * LANES, LANES), BF16),
            pltpu.VMEM((2 * LANES, 2 * WIDE), BF16),
            pltpu.VMEM((2 * STEPS, WIDE), F32),
            pltpu.VMEM((1, STN), jnp.int32),
            pltpu.VMEM((1, STN), jnp.int32),
            pltpu.SMEM((NF,), F32),
            pltpu.SMEM((NF,), F32),
            pltpu.SMEM((NF, NF), F32),
            pltpu.SMEM((NF,), F32),
            pltpu.SMEM((STEPS,), jnp.int32),
            pltpu.VMEM((STEPS, N_ROW, CAP, LANES), F32),
            pltpu.VMEM((N_ROW, STEPS, CAP, LANES), F32),
            pltpu.VMEM((SLOTS // 2, WIDE), F32),
            dma((11,)),
            dma((STEPS, 2, CHUNKS)),
            dma((STEPS, 2, CHUNKS)),
            dma((STEPS, CHUNKS)),
            dma((STEPS, CHUNKS)),
            dma((STEPS, 2)),
            dma((STEPS, 2)),
            dma((2, N_ROW)),
            dma((2, N_ROW)),
        ],
        compiler_params=pltpu.CompilerParams(
            collective_id=0, has_side_effects=True, vmem_limit_bytes=40 * 1024 * 1024
        ),
    )(
        *(
            pltpu.with_memory_space_constraint(operand, pltpu.HBM)
            for operand in (
                conserved,
                diffusivity,
                axial_speed,
                coupling,
                weights,
                window,
                station_cell.reshape(1, STN),
                owner_row.reshape(1, STN),
                jnp.asarray(azimuth_tables()),
                jnp.asarray(spread_table()),
                jnp.asarray(phase_rows()),
            )
        )
    )
    return advanced, spectra[None]


def solution(mesh):
    in_specs = (
        P(None, "gx", "row", "ta"),
        P(),
        P(),
        P(),
        P(),
        P(("gx", "row")),
        P(("gx", "row"), None),
        P(),
    )
    out_specs = (P(None, "gx", "row", "ta"), P(("gx", "row"), "ta", None))
    return jax.shard_map(
        functools.partial(local, mesh.shape["gx"]),
        mesh=mesh,
        in_specs=in_specs,
        out_specs=out_specs,
        check_vma=False,
    )
```

```python
import functools
import math

import jax
import jax.numpy as jnp
import numpy as np
from jax import lax
from jax.experimental import pallas as pl
from jax.experimental.pallas import tpu as pltpu
from jax.sharding import PartitionSpec as P

NF = 5
CX = 8
CR = 32
LANES = 128
NTH = 256
NM = 33
NFREQ = 16
STEPS = 4
CAP = 16
STN = 32
N_ROW = 8
SLOTS = N_ROW * CAP
HALF = SLOTS // 2
COLS = NFREQ * 2 * NM
WIDE = 1152
MESH = pl.DeviceIdType.MESH
F32 = jnp.float32
BF16 = jnp.bfloat16
ORDER = (0, 3, 1, 2)
CHUNKS = 4


def split(value):
    high = value.astype(BF16)
    return high, (value - high.astype(F32)).astype(BF16)


def in_pieces(table, axis):
    high = table.astype(jnp.bfloat16)
    low = (table - high.astype(np.float32)).astype(jnp.bfloat16)
    return np.concatenate([high, high, low], axis=axis)


def lane_of(t, part, m):
    return (0 if t == STEPS - 1 else 2 * NM * t) + NM * part + m


def azimuth_tables():
    theta = np.arange(NTH)
    turns = theta[:, None] * np.arange(NM)[None, :] % NTH
    angle = 2.0 * math.pi / NTH * turns
    table = np.zeros((STEPS, NTH, 2 * LANES), np.float32)
    for t in range(STEPS):
        table[t, :, lane_of(t, 0, 0) : lane_of(t, 0, NM)] = np.cos(angle) / math.sqrt(NTH)
        table[t, :, lane_of(t, 1, 0) : lane_of(t, 1, NM)] = np.sin(angle) / math.sqrt(NTH)
    table = table.reshape(STEPS, 2, LANES, 2 * LANES).swapaxes(0, 1)
    return in_pieces(table, 2)


def phase_tables():
    early = np.zeros((2 * LANES, WIDE), np.float32)
    late = np.zeros((LANES, WIDE), np.float32)
    for t in range(STEPS):
        rows = late if t == STEPS - 1 else early
        for k in range(NFREQ):
            phase = math.pi * (k + 1) * t / NFREQ
            for m in range(NM):
                first, second = (k * 2) * NM + m, (k * 2 + 1) * NM + m
                rows[lane_of(t, 0, m), first] = math.cos(phase)
                rows[lane_of(t, 1, m), first] = -math.sin(phase)
                rows[lane_of(t, 0, m), second] = -math.sin(phase)
                rows[lane_of(t, 1, m), second] = -math.cos(phase)
    return in_pieces(early, 0), in_pieces(late, 0)


def kernel(
    n_gx,
    x_ref,
    diffusivity_hbm,
    axial_speed_hbm,
    coupling_hbm,
    weights_hbm,
    window_hbm,
    cell_hbm,
    owner_hbm,
    table_hbm,
    early_hbm,
    late_hbm,
    out_ref,
    spectra_ref,
    s0,
    s1,
    s2,
    s3,
    mirror,
    row_out,
    row_in,
    pressure,
    place,
    table,
    early,
    late,
    cell_ref,
    owner_ref,
    diffusivity,
    axial_speed,
    coupling,
    weights,
    window,
    z_early,
    z_late,
    half_early,
    half_late,
    sum_early,
    sum_late,
    in_early,
    in_late,
    acc,
    ready,
    local_sem,
    gx_send,
    gx_recv,
    ta_send,
    ta_recv,
    row_send,
    row_recv,
    half_send,
    half_recv,
    z_send,
    z_recv,
):
    g, j, ta = lax.axis_index("gx"), lax.axis_index("row"), lax.axis_index("ta")
    other = 1 - ta
    state = (s0, s1, s2, s3)
    has = {("gx", 0): g > 0, ("gx", 1): g < n_gx - 1, ("row", 0): j > 0, ("row", 1): j < N_ROW - 1}
    to = {
        ("gx", 0): (g - 1, j, ta),
        ("gx", 1): (g + 1, j, ta),
        ("row", 0): (g, j - 1, ta),
        ("row", 1): (g, j + 1, ta),
    }

    loads = [
        pltpu.make_async_copy(x_ref, s0.at[:, 2 : 2 + CX, 8 : 8 + CR, :], local_sem.at[0]),
        pltpu.make_async_copy(table_hbm.at[ta], table, local_sem.at[1]),
        pltpu.make_async_copy(early_hbm, early, local_sem.at[2]),
        pltpu.make_async_copy(late_hbm, late, local_sem.at[3]),
        pltpu.make_async_copy(cell_hbm, cell_ref, local_sem.at[4]),
        pltpu.make_async_copy(owner_hbm, owner_ref, local_sem.at[5]),
        pltpu.make_async_copy(diffusivity_hbm, diffusivity, local_sem.at[6]),
        pltpu.make_async_copy(axial_speed_hbm, axial_speed, local_sem.at[7]),
        pltpu.make_async_copy(coupling_hbm, coupling, local_sem.at[8]),
        pltpu.make_async_copy(weights_hbm, weights, local_sem.at[9]),
        pltpu.make_async_copy(window_hbm, window, local_sem.at[10]),
    ]
    for load in loads:
        load.start()

    barrier = pltpu.get_barrier_semaphore()
    sides = (("gx", 0), ("gx", 1), ("row", 0), ("row", 1))
    for key in sides:

        @pl.when(has[key])
        def _():
            pl.semaphore_signal(barrier, 1, device_id=to[key], device_id_type=MESH)

    pl.semaphore_signal(barrier, 1, device_id=(g, j, other), device_id_type=MESH)

    def in_range(distance):
        return (j - distance >= 0, j - distance), (j + distance < N_ROW, j + distance)

    def announce(distance):
        for inside, owner in in_range(distance):

            @pl.when(inside)
            def _():
                pl.semaphore_signal(
                    ready.at[distance // 2], 1, device_id=(g, owner, ta), device_id_type=MESH
                )

        if distance == 1:
            pl.semaphore_signal(ready.at[0], 1, device_id=(g, j, other), device_id_type=MESH)

    def heard(distance):
        count = 1 if distance == 1 else 0
        for inside, _ in in_range(distance):
            count = count + jnp.where(inside, 1, 0)
        pl.semaphore_wait(ready.at[distance // 2], count)

    for side in range(2):

        @pl.when(jnp.logical_not(has["gx", side]))
        def _():
            for s in state:
                s[:, 10 * side : 10 * side + 2, 8 : 8 + CR, :] = jnp.zeros((NF, 2, CR, LANES), F32)

        @pl.when(jnp.logical_not(has["row", side]))
        def _():
            for t in range(STEPS):
                row_in[t, side] = jnp.zeros((NF, CX, 2, LANES), F32)

    loads[0].wait()
    for f in range(NF):
        row_out[0, 0, f] = s0[f, 2 : 2 + CX, 8:10, :]
        row_out[0, 1, f] = s0[f, 2 : 2 + CX, 38:40, :]

    def gx_copy(t, side, c):
        rows = pl.ds(8 + 8 * c, 8)
        return pltpu.make_async_remote_copy(
            src_ref=state[t].at[:, pl.ds(8 * side - 2 * side + 2, 2), rows, :],
            dst_ref=state[t].at[:, pl.ds(10 - 10 * side, 2), rows, :],
            send_sem=gx_send.at[t, side, c],
            recv_sem=gx_recv.at[t, 1 - side, c],
            device_id=to["gx", side],
            device_id_type=MESH,
        )

    def gx_wait(t, side, c):
        rows = pl.ds(8 + 8 * c, 8)
        return pltpu.make_async_remote_copy(
            src_ref=state[t].at[:, pl.ds(2, 2), rows, :],
            dst_ref=state[t].at[:, pl.ds(10 * side, 2), rows, :],
            send_sem=gx_send.at[t, side, c],
            recv_sem=gx_recv.at[t, side, c],
            device_id=to["gx", side],
            device_id_type=MESH,
        )

    def row_copy(t, side):
        return pltpu.make_async_remote_copy(
            src_ref=row_out.at[t, side],
            dst_ref=row_in.at[t, 1 - side],
            send_sem=row_send.at[t, side],
            recv_sem=row_recv.at[t, 1 - side],
            device_id=to["row", side],
            device_id_type=MESH,
        )

    def row_wait(t, side):
        return pltpu.make_async_remote_copy(
            src_ref=row_out.at[t, side],
            dst_ref=row_in.at[t, side],
            send_sem=row_send.at[t, side],
            recv_sem=row_recv.at[t, side],
            device_id=to["row", side],
            device_id_type=MESH,
        )

    def ta_copy(t, c):
        return pltpu.make_async_remote_copy(
            src_ref=state[t].at[:, 2 : 2 + CX, pl.ds(8 + 8 * c, 8), :],
            dst_ref=mirror.at[t, :, :, pl.ds(8 * c, 8), :],
            send_sem=ta_send.at[t, c],
            recv_sem=ta_recv.at[t, c],
            device_id=(g, j, other),
            device_id_type=MESH,
        )

    def send_chunk(t, c):
        for side, edge in ((0, 0), (1, CHUNKS - 1)):
            if c == edge:
                pl.when(has["row", side])(row_copy(t, side).start)
        for side in range(2):
            pl.when(has["gx", side])(gx_copy(t, side, c).start)
        ta_copy(t, c).start()

    peers = 1
    for key in sides:
        peers = peers + jnp.where(has[key], 1, 0)
    pl.semaphore_wait(barrier, peers)
    for c in ORDER:
        send_chunk(0, c)
    announce(1)

    for load in loads[1:]:
        load.wait()

    eye = lax.broadcasted_iota(jnp.int32, (STN, STN), 0) == lax.broadcasted_iota(jnp.int32, (STN, STN), 1)
    before = lax.broadcasted_iota(jnp.int32, (STN, STN), 0) < lax.broadcasted_iota(jnp.int32, (STN, STN), 1)
    owners = owner_ref[...]
    owner_across = jnp.broadcast_to(owners, (STN, STN)).astype(F32)
    owner_down = jnp.sum(jnp.where(eye, owner_across, 0.0), axis=1, keepdims=True)
    same = jnp.logical_and(before, owner_down == owner_across)
    rank = jnp.sum(jnp.where(same, 1.0, 0.0), axis=0, keepdims=True)
    slot = ((owners % 2) * HALF + (owners // 2) * CAP).astype(F32) + rank
    slots = lax.broadcasted_iota(jnp.int32, (SLOTS, STN), 0).astype(F32)
    slot_onehot = jnp.where(slots == slot, 1.0, 0.0).astype(BF16)
    station = cell_ref[...]
    local_cell = (station // (CR * N_ROW) - g * CX) * CR + (station % (CR * N_ROW) - j * CR)
    cell_across = jnp.broadcast_to(local_cell, (STN, STN)).astype(F32)
    cell_down = jnp.sum(jnp.where(eye, cell_across, 0.0), axis=1, keepdims=True)
    cells = lax.broadcasted_iota(jnp.int32, (STN, CX * CR), 1).astype(F32)
    cell_onehot = jnp.where(cells == cell_down, 1.0, 0.0).astype(BF16)
    place[...] = jnp.dot(slot_onehot, cell_onehot, preferred_element_type=F32).astype(BF16)

    lane = lax.broadcasted_iota(jnp.int32, (8, LANES), 1)
    first1, first2 = lane < 1, lane < 2
    last1, last2 = lane >= LANES - 1, lane >= LANES - 2
    rate = [diffusivity[f] * (1.0 / 12.0) for f in range(NF)]
    velocity = [axial_speed[f] * (1.0 / 12.0) for f in range(NF)]
    mix = [
        [coupling[f, h] + (1.0 - 7.5 * diffusivity[f] if f == h else 0.0) for h in range(NF)]
        for f in range(NF)
    ]
    press = [weights[f] for f in range(NF)]

    def step_chunk(t, c):
        s = state[t]
        r0 = 8 + 8 * c

        def body(x, carry):
            center = [s[f, x + 2, r0 : r0 + 8, :] for f in range(NF)]
            total = None
            for f in range(NF):
                v = center[f]
                o = mirror[t, f, x, 8 * c : 8 * c + 8, :]
                up1, up2 = s[f, x + 3, r0 : r0 + 8, :], s[f, x + 4, r0 : r0 + 8, :]
                dn1, dn2 = s[f, x + 1, r0 : r0 + 8, :], s[f, x, r0 : r0 + 8, :]
                near = (up1 + dn1) + (s[f, x + 2, r0 + 1 : r0 + 9, :] + s[f, x + 2, r0 - 1 : r0 + 7, :])
                far = (up2 + dn2) + (s[f, x + 2, r0 + 2 : r0 + 10, :] + s[f, x + 2, r0 - 2 : r0 + 6, :])
                near = near + (
                    pltpu.roll(jnp.where(first1, o, v), LANES - 1, 1)
                    + pltpu.roll(jnp.where(last1, o, v), 1, 1)
                )
                far = far + (
                    pltpu.roll(jnp.where(first2, o, v), LANES - 2, 1)
                    + pltpu.roll(jnp.where(last2, o, v), 2, 1)
                )
                gradient = 8.0 * (up1 - dn1) - (up2 - dn2)
                new = rate[f] * (16.0 * near - far) - velocity[f] * gradient
                for h in range(NF):
                    new = new + mix[f][h] * center[h]
                if t < STEPS - 1:
                    state[t + 1][f, x + 2, r0 : r0 + 8, :] = new
                    if c == 0:
                        row_out[t + 1, 0, f, x] = new[0:2]
                    if c == CHUNKS - 1:
                        row_out[t + 1, 1, f, x] = new[6:8]
                else:
                    out_ref[f, x, 8 * c : 8 * c + 8, :] = new
                part = press[f] * new
                total = part if total is None else total + part
            pressure[pl.ds(x * CR + 8 * c, 8), :] = total
            return carry

        lax.fori_loop(0, CX, body, 0, unroll=True)

    def coefficients(t):
        high, low = split(pressure[...])
        both = jnp.dot(place[...], jnp.concatenate([high, low], axis=1), preferred_element_type=F32)
        high, low = split(both[:, :LANES] + both[:, LANES:])
        pieces = jnp.concatenate([high, low, high], axis=1)
        if t == STEPS - 1:
            z_late[...] = jnp.dot(pieces, table[t, :, :LANES], preferred_element_type=F32)
        else:
            new = jnp.dot(pieces, table[t], preferred_element_type=F32)
            z_early[...] = new if t == 0 else z_early[...] + new

    half = j // (N_ROW // 2)
    source = j % (N_ROW // 2)
    stages = ((z_early, half_early, sum_early, in_early), (z_late, half_late, sum_late, in_late))

    def half_copy(stage):
        whole, arrived, _, _ = stages[stage]
        return pltpu.make_async_remote_copy(
            src_ref=whole.at[pl.ds(pl.multiple_of(other * HALF, HALF), HALF)],
            dst_ref=arrived,
            send_sem=half_send.at[stage],
            recv_sem=half_recv.at[stage],
            device_id=(g, j, other),
            device_id_type=MESH,
        )

    def z_copy(stage, i):
        _, _, summed, landing = stages[stage]
        return pltpu.make_async_remote_copy(
            src_ref=summed.at[i],
            dst_ref=landing.at[source],
            send_sem=z_send.at[stage, i],
            recv_sem=z_recv.at[stage, source],
            device_id=(g, 2 * i + ta, half),
            device_id_type=MESH,
        )

    def away(i):
        return jnp.logical_or(2 * i + ta != j, half != ta)

    def z_start(stage):
        whole, arrived, summed, landing = stages[stage]
        half_copy(stage).wait_recv()
        own = whole[pl.ds(pl.multiple_of(ta * HALF, HALF), HALF), :]
        summed[...] = (own + arrived[...]).reshape(summed.shape)
        for ahead in range(N_ROW // 2):
            i = lax.rem(j // 2 + 2 + ahead, N_ROW // 2)
            pl.when(away(i))(z_copy(stage, i).start)

        @pl.when(jnp.logical_not(away(j // 2)))
        def _():
            landing[source] = summed[j // 2]

    def z_wait(stage):
        _, _, summed, landing = stages[stage]
        for src in range(N_ROW // 2):
            copy = pltpu.make_async_remote_copy(
                src_ref=summed.at[0],
                dst_ref=landing.at[src],
                send_sem=z_send.at[stage, 0],
                recv_sem=z_recv.at[stage, src],
                device_id=(g, j, other),
                device_id_type=MESH,
            )
            mine = jnp.logical_and(
                jnp.logical_and(half == ta, source == src), j % 2 == ta
            )
            pl.when(jnp.logical_not(mine))(copy.wait_recv)

    w = [window[t].astype(F32) * 0.125 for t in range(STEPS)]

    def accumulate_early():
        z = in_early[...].reshape(HALF, 2 * LANES)
        lanes = lax.broadcasted_iota(jnp.int32, (1, 2 * LANES), 1)
        scale = jnp.where(lanes < 2 * NM, w[0], jnp.where(lanes < 4 * NM, w[1], w[2]))
        high, low = split(z * scale)
        pieces = jnp.concatenate([high, low, high], axis=1)
        return jnp.dot(pieces, early[...], preferred_element_type=F32)

    def accumulate_late():
        high, low = split(in_late[...].reshape(HALF, LANES) * w[STEPS - 1])
        pieces = jnp.concatenate([high, low, high], axis=1)
        return jnp.dot(pieces, late[...], preferred_element_type=F32)

    for t in range(STEPS):
        for c in ORDER:
            for side, edge in ((0, 0), (1, CHUNKS - 1)):
                if c == edge:
                    pl.when(has["row", side])(row_wait(t, side).wait_recv)
                    at = 6 if side == 0 else 8 + CR
                    for f in range(NF):
                        state[t][f, 2 : 2 + CX, at : at + 2, :] = row_in[t, side, f]
            for side in range(2):
                pl.when(has["gx", side])(gx_wait(t, side, c).wait_recv)
            ta_copy(t, c).wait_recv()
            step_chunk(t, c)
            if t < STEPS - 1:
                send_chunk(t + 1, c)
            elif c == ORDER[1]:
                z_start(0)
        coefficients(t)
        if t < STEPS - 1:
            heard(1 << t)
        if t < STEPS - 2:
            announce(2 << t)
        if t == STEPS - 2:
            half_copy(0).start()
    half_copy(1).start()
    z_start(1)
    z_wait(0)
    acc[...] = accumulate_early()
    for t in range(STEPS):
        for c in range(CHUNKS):
            for side in range(2):
                pl.when(has["gx", side])(gx_copy(t, side, c).wait_send)
            ta_copy(t, c).wait_send()
        for side in range(2):
            pl.when(has["row", side])(row_copy(t, side).wait_send)
    for stage in range(2):
        half_copy(stage).wait_send()
        for i in range(N_ROW // 2):
            pl.when(away(i))(z_copy(stage, i).wait_send)
    z_wait(1)
    spectra_ref[...] = (acc[...] + accumulate_late())[:, :COLS]


def local(n_gx, conserved, diffusivity, axial_speed, coupling, weights, station_cell, owner_row, window):
    vmem = pl.BlockSpec(memory_space=pltpu.VMEM)
    hbm = pl.BlockSpec(memory_space=pltpu.HBM)
    big = pltpu.VMEM((NF, CX + 4, CR + 16, LANES), F32)
    dma = pltpu.SemaphoreType.DMA
    advanced, spectra = pl.pallas_call(
        functools.partial(kernel, n_gx),
        out_shape=(
            jax.ShapeDtypeStruct((NF, CX, CR, LANES), F32),
            jax.ShapeDtypeStruct((SLOTS // 2, COLS), F32),
        ),
        in_specs=[hbm] * 11,
        out_specs=(vmem, vmem),
        scratch_shapes=[
            big,
            big,
            big,
            big,
            pltpu.VMEM((STEPS, NF, CX, CR, LANES), F32),
            pltpu.VMEM((STEPS, 2, NF, CX, 2, LANES), F32),
            pltpu.VMEM((STEPS, 2, NF, CX, 2, LANES), F32),
            pltpu.VMEM((CX * CR, LANES), F32),
            pltpu.VMEM((SLOTS, CX * CR), BF16),
            pltpu.VMEM((STEPS, 3 * LANES, 2 * LANES), BF16),
            pltpu.VMEM((6 * LANES, WIDE), BF16),
            pltpu.VMEM((3 * LANES, WIDE), BF16),
            pltpu.VMEM((1, STN), jnp.int32),
            pltpu.VMEM((1, STN), jnp.int32),
            pltpu.SMEM((NF,), F32),
            pltpu.SMEM((NF,), F32),
            pltpu.SMEM((NF, NF), F32),
            pltpu.SMEM((NF,), F32),
            pltpu.SMEM((STEPS,), jnp.int32),
            pltpu.VMEM((SLOTS, 2 * LANES), F32),
            pltpu.VMEM((SLOTS, LANES), F32),
            pltpu.VMEM((HALF, 2 * LANES), F32),
            pltpu.VMEM((HALF, LANES), F32),
            pltpu.VMEM((N_ROW // 2, CAP, 2 * LANES), F32),
            pltpu.VMEM((N_ROW // 2, CAP, LANES), F32),
            pltpu.VMEM((N_ROW // 2, CAP, 2 * LANES), F32),
            pltpu.VMEM((N_ROW // 2, CAP, LANES), F32),
            pltpu.VMEM((HALF, WIDE), F32),
            pltpu.SemaphoreType.REGULAR((3,)),
            dma((11,)),
            dma((STEPS, 2, CHUNKS)),
            dma((STEPS, 2, CHUNKS)),
            dma((STEPS, CHUNKS)),
            dma((STEPS, CHUNKS)),
            dma((STEPS, 2)),
            dma((STEPS, 2)),
            dma((2,)),
            dma((2,)),
            dma((2, N_ROW // 2)),
            dma((2, N_ROW // 2)),
        ],
        compiler_params=pltpu.CompilerParams(
            collective_id=0, has_side_effects=True, vmem_limit_bytes=40 * 1024 * 1024
        ),
    )(
        *(
            pltpu.with_memory_space_constraint(operand, pltpu.HBM)
            for operand in (
                conserved,
                diffusivity,
                axial_speed,
                coupling,
                weights,
                window,
                station_cell.reshape(1, STN),
                owner_row.reshape(1, STN),
                jnp.asarray(azimuth_tables()),
                *(jnp.asarray(table) for table in phase_tables()),
            )
        )
    )
    return advanced, spectra[None]


def solution(mesh):
    in_specs = (
        P(None, "gx", "row", "ta"),
        P(),
        P(),
        P(),
        P(),
        P(("gx", "row")),
        P(("gx", "row"), None),
        P(),
    )
    out_specs = (P(None, "gx", "row", "ta"), P(("gx", "row"), "ta", None))
    return jax.shard_map(
        functools.partial(local, mesh.shape["gx"]),
        mesh=mesh,
        in_specs=in_specs,
        out_specs=out_specs,
        check_vma=False,
    )
```

```python
import functools
import math

import jax
import jax.numpy as jnp
import numpy as np
from jax import lax
from jax.experimental import pallas as pl
from jax.experimental.pallas import tpu as pltpu
from jax.sharding import PartitionSpec as P

NF = 5
CX = 8
CR = 32
LANES = 128
NTH = 256
NM = 33
NFREQ = 16
STEPS = 4
CAP = 16
STN = 32
N_ROW = 8
SLOTS = N_ROW * CAP
HALF = SLOTS // 2
COLS = NFREQ * 2 * NM
WIDE = 1152
MESH = pl.DeviceIdType.MESH
F32 = jnp.float32
BF16 = jnp.bfloat16
ORDER = (0, 3, 1, 2)
CHUNKS = 4


def split(value):
    high = value.astype(BF16)
    return high, (value - high.astype(F32)).astype(BF16)


def in_pieces(table, axis):
    high = table.astype(jnp.bfloat16)
    low = (table - high.astype(np.float32)).astype(jnp.bfloat16)
    return np.concatenate([high, high, low], axis=axis)


def lane_of(t, part, m):
    return (0 if t == STEPS - 1 else 2 * NM * t) + NM * part + m


def azimuth_tables():
    theta = np.arange(NTH)
    turns = theta[:, None] * np.arange(NM)[None, :] % NTH
    angle = 2.0 * math.pi / NTH * turns
    table = np.zeros((STEPS, NTH, 2 * LANES), np.float32)
    for t in range(STEPS):
        table[t, :, lane_of(t, 0, 0) : lane_of(t, 0, NM)] = np.cos(angle) / math.sqrt(NTH)
        table[t, :, lane_of(t, 1, 0) : lane_of(t, 1, NM)] = np.sin(angle) / math.sqrt(NTH)
    table = table.reshape(STEPS, 2, LANES, 2 * LANES).swapaxes(0, 1)
    return in_pieces(table, 2)


def phase_tables():
    early = np.zeros((2 * LANES, WIDE), np.float32)
    late = np.zeros((LANES, WIDE), np.float32)
    for t in range(STEPS):
        rows = late if t == STEPS - 1 else early
        for k in range(NFREQ):
            phase = math.pi * (k + 1) * t / NFREQ
            for m in range(NM):
                first, second = (k * 2) * NM + m, (k * 2 + 1) * NM + m
                rows[lane_of(t, 0, m), first] = math.cos(phase)
                rows[lane_of(t, 1, m), first] = -math.sin(phase)
                rows[lane_of(t, 0, m), second] = -math.sin(phase)
                rows[lane_of(t, 1, m), second] = -math.cos(phase)
    return in_pieces(early, 0), in_pieces(late, 0)


def kernel(
    n_gx,
    x_ref,
    diffusivity_hbm,
    axial_speed_hbm,
    coupling_hbm,
    weights_hbm,
    window_hbm,
    cell_hbm,
    owner_hbm,
    table_hbm,
    early_hbm,
    late_hbm,
    out_ref,
    spectra_ref,
    s0,
    s1,
    s2,
    s3,
    mirror,
    row_out,
    row_in,
    pressure,
    place,
    table,
    early,
    late,
    cell_ref,
    owner_ref,
    diffusivity,
    axial_speed,
    coupling,
    weights,
    window,
    z_early,
    z_late,
    half_early,
    half_late,
    sum_early,
    sum_late,
    in_early,
    in_late,
    acc,
    ready,
    local_sem,
    gx_send,
    gx_recv,
    ta_send,
    ta_recv,
    row_send,
    row_recv,
    half_send,
    half_recv,
    z_send,
    z_recv,
):
    g, j, ta = lax.axis_index("gx"), lax.axis_index("row"), lax.axis_index("ta")
    other = 1 - ta
    state = (s0, s1, s2, s3)
    has = {("gx", 0): g > 0, ("gx", 1): g < n_gx - 1, ("row", 0): j > 0, ("row", 1): j < N_ROW - 1}
    to = {
        ("gx", 0): (g - 1, j, ta),
        ("gx", 1): (g + 1, j, ta),
        ("row", 0): (g, j - 1, ta),
        ("row", 1): (g, j + 1, ta),
    }

    loads = [
        pltpu.make_async_copy(x_ref, s0.at[:, 2 : 2 + CX, 8 : 8 + CR, :], local_sem.at[0]),
        pltpu.make_async_copy(table_hbm.at[ta], table, local_sem.at[1]),
        pltpu.make_async_copy(early_hbm, early, local_sem.at[2]),
        pltpu.make_async_copy(late_hbm, late, local_sem.at[3]),
        pltpu.make_async_copy(cell_hbm, cell_ref, local_sem.at[4]),
        pltpu.make_async_copy(owner_hbm, owner_ref, local_sem.at[5]),
        pltpu.make_async_copy(diffusivity_hbm, diffusivity, local_sem.at[6]),
        pltpu.make_async_copy(axial_speed_hbm, axial_speed, local_sem.at[7]),
        pltpu.make_async_copy(coupling_hbm, coupling, local_sem.at[8]),
        pltpu.make_async_copy(weights_hbm, weights, local_sem.at[9]),
        pltpu.make_async_copy(window_hbm, window, local_sem.at[10]),
    ]
    for load in loads:
        load.start()

    barrier = pltpu.get_barrier_semaphore()
    sides = (("gx", 0), ("gx", 1), ("row", 0), ("row", 1))
    for key in sides:

        @pl.when(has[key])
        def _():
            pl.semaphore_signal(barrier, 1, device_id=to[key], device_id_type=MESH)

    pl.semaphore_signal(barrier, 1, device_id=(g, j, other), device_id_type=MESH)

    def in_range(distance):
        return (j - distance >= 0, j - distance), (j + distance < N_ROW, j + distance)

    def announce(distance):
        for inside, owner in in_range(distance):

            @pl.when(inside)
            def _():
                pl.semaphore_signal(
                    ready.at[distance // 2], 1, device_id=(g, owner, ta), device_id_type=MESH
                )

        if distance == 1:
            pl.semaphore_signal(ready.at[0], 1, device_id=(g, j, other), device_id_type=MESH)

    def heard(distance):
        count = 1 if distance == 1 else 0
        for inside, _ in in_range(distance):
            count = count + jnp.where(inside, 1, 0)
        pl.semaphore_wait(ready.at[distance // 2], count)

    for side in range(2):

        @pl.when(jnp.logical_not(has["gx", side]))
        def _():
            for s in state:
                s[:, 10 * side : 10 * side + 2, 8 : 8 + CR, :] = jnp.zeros((NF, 2, CR, LANES), F32)

        @pl.when(jnp.logical_not(has["row", side]))
        def _():
            for t in range(STEPS):
                row_in[t, side] = jnp.zeros((NF, CX, 2, LANES), F32)


    def gx_copy(t, side, c):
        rows = pl.ds(8 + 8 * c, 8)
        return pltpu.make_async_remote_copy(
            src_ref=state[t].at[:, pl.ds(8 * side - 2 * side + 2, 2), rows, :],
            dst_ref=state[t].at[:, pl.ds(10 - 10 * side, 2), rows, :],
            send_sem=gx_send.at[t, side, c],
            recv_sem=gx_recv.at[t, 1 - side, c],
            device_id=to["gx", side],
            device_id_type=MESH,
        )

    def gx_wait(t, side, c):
        rows = pl.ds(8 + 8 * c, 8)
        return pltpu.make_async_remote_copy(
            src_ref=state[t].at[:, pl.ds(2, 2), rows, :],
            dst_ref=state[t].at[:, pl.ds(10 * side, 2), rows, :],
            send_sem=gx_send.at[t, side, c],
            recv_sem=gx_recv.at[t, side, c],
            device_id=to["gx", side],
            device_id_type=MESH,
        )

    def row_copy(t, side):
        return pltpu.make_async_remote_copy(
            src_ref=x_ref.at[:, :, pl.ds((CR - 2) * side, 2), :] if t == 0 else row_out.at[t, side],
            dst_ref=row_in.at[t, 1 - side],
            send_sem=row_send.at[t, side],
            recv_sem=row_recv.at[t, 1 - side],
            device_id=to["row", side],
            device_id_type=MESH,
        )

    def row_wait(t, side):
        return pltpu.make_async_remote_copy(
            src_ref=row_out.at[t, side],
            dst_ref=row_in.at[t, side],
            send_sem=row_send.at[t, side],
            recv_sem=row_recv.at[t, side],
            device_id=to["row", side],
            device_id_type=MESH,
        )

    def ta_copy(t, c):
        return pltpu.make_async_remote_copy(
            src_ref=state[t].at[:, 2 : 2 + CX, pl.ds(8 + 8 * c, 8), :],
            dst_ref=mirror.at[t, :, :, pl.ds(8 * c, 8), :],
            send_sem=ta_send.at[t, c],
            recv_sem=ta_recv.at[t, c],
            device_id=(g, j, other),
            device_id_type=MESH,
        )

    def send_chunk(t, c):
        for side, edge in ((0, 0), (1, CHUNKS - 1)):
            if c == edge and t > 0:
                pl.when(has["row", side])(row_copy(t, side).start)
        for side in range(2):
            pl.when(has["gx", side])(gx_copy(t, side, c).start)
        ta_copy(t, c).start()

    peers = 1
    for key in sides:
        peers = peers + jnp.where(has[key], 1, 0)
    pl.semaphore_wait(barrier, peers)
    for side in range(2):
        pl.when(has["row", side])(row_copy(0, side).start)
    loads[0].wait()
    for c in ORDER:
        send_chunk(0, c)
    announce(1)

    for load in loads[1:]:
        load.wait()

    eye = lax.broadcasted_iota(jnp.int32, (STN, STN), 0) == lax.broadcasted_iota(jnp.int32, (STN, STN), 1)
    before = lax.broadcasted_iota(jnp.int32, (STN, STN), 0) < lax.broadcasted_iota(jnp.int32, (STN, STN), 1)
    owners = owner_ref[...]
    owner_across = jnp.broadcast_to(owners, (STN, STN)).astype(F32)
    owner_down = jnp.sum(jnp.where(eye, owner_across, 0.0), axis=1, keepdims=True)
    same = jnp.logical_and(before, owner_down == owner_across)
    rank = jnp.sum(jnp.where(same, 1.0, 0.0), axis=0, keepdims=True)
    slot = ((owners % 2) * HALF + (owners // 2) * CAP).astype(F32) + rank
    slots = lax.broadcasted_iota(jnp.int32, (SLOTS, STN), 0).astype(F32)
    slot_onehot = jnp.where(slots == slot, 1.0, 0.0).astype(BF16)
    station = cell_ref[...]
    local_cell = (station // (CR * N_ROW) - g * CX) * CR + (station % (CR * N_ROW) - j * CR)
    cell_across = jnp.broadcast_to(local_cell, (STN, STN)).astype(F32)
    cell_down = jnp.sum(jnp.where(eye, cell_across, 0.0), axis=1, keepdims=True)
    cells = lax.broadcasted_iota(jnp.int32, (STN, CX * CR), 1).astype(F32)
    cell_onehot = jnp.where(cells == cell_down, 1.0, 0.0).astype(BF16)
    place[...] = jnp.dot(slot_onehot, cell_onehot, preferred_element_type=F32).astype(BF16)

    lane = lax.broadcasted_iota(jnp.int32, (8, LANES), 1)
    first1, first2 = lane < 1, lane < 2
    last1, last2 = lane >= LANES - 1, lane >= LANES - 2
    rate = [diffusivity[f] * (1.0 / 12.0) for f in range(NF)]
    velocity = [axial_speed[f] * (1.0 / 12.0) for f in range(NF)]
    mix = [
        [coupling[f, h] + (1.0 - 7.5 * diffusivity[f] if f == h else 0.0) for h in range(NF)]
        for f in range(NF)
    ]
    press = [weights[f] for f in range(NF)]

    def step_chunk(t, c):
        s = state[t]
        r0 = 8 + 8 * c

        def body(x, carry):
            center = [s[f, x + 2, r0 : r0 + 8, :] for f in range(NF)]
            total = None
            for f in range(NF):
                v = center[f]
                o = mirror[t, f, x, 8 * c : 8 * c + 8, :]
                up1, up2 = s[f, x + 3, r0 : r0 + 8, :], s[f, x + 4, r0 : r0 + 8, :]
                dn1, dn2 = s[f, x + 1, r0 : r0 + 8, :], s[f, x, r0 : r0 + 8, :]
                near = (up1 + dn1) + (s[f, x + 2, r0 + 1 : r0 + 9, :] + s[f, x + 2, r0 - 1 : r0 + 7, :])
                far = (up2 + dn2) + (s[f, x + 2, r0 + 2 : r0 + 10, :] + s[f, x + 2, r0 - 2 : r0 + 6, :])
                near = near + (
                    pltpu.roll(jnp.where(first1, o, v), LANES - 1, 1)
                    + pltpu.roll(jnp.where(last1, o, v), 1, 1)
                )
                far = far + (
                    pltpu.roll(jnp.where(first2, o, v), LANES - 2, 1)
                    + pltpu.roll(jnp.where(last2, o, v), 2, 1)
                )
                gradient = 8.0 * (up1 - dn1) - (up2 - dn2)
                new = rate[f] * (16.0 * near - far) - velocity[f] * gradient
                for h in range(NF):
                    new = new + mix[f][h] * center[h]
                if t < STEPS - 1:
                    state[t + 1][f, x + 2, r0 : r0 + 8, :] = new
                    if c == 0:
                        row_out[t + 1, 0, f, x] = new[0:2]
                    if c == CHUNKS - 1:
                        row_out[t + 1, 1, f, x] = new[6:8]
                else:
                    out_ref[f, x, 8 * c : 8 * c + 8, :] = new
                part = press[f] * new
                total = part if total is None else total + part
            pressure[pl.ds(x * CR + 8 * c, 8), :] = total
            return carry

        lax.fori_loop(0, CX, body, 0, unroll=True)

    def coefficients(t):
        high, low = split(pressure[...])
        both = jnp.dot(place[...], jnp.concatenate([high, low], axis=1), preferred_element_type=F32)
        high, low = split(both[:, :LANES] + both[:, LANES:])
        pieces = jnp.concatenate([high, low, high], axis=1)
        if t == STEPS - 1:
            z_late[...] = jnp.dot(pieces, table[t, :, :LANES], preferred_element_type=F32)
        else:
            new = jnp.dot(pieces, table[t], preferred_element_type=F32)
            z_early[...] = new if t == 0 else z_early[...] + new

    half = j // (N_ROW // 2)
    source = j % (N_ROW // 2)
    stages = ((z_early, half_early, sum_early, in_early), (z_late, half_late, sum_late, in_late))

    def half_copy(stage):
        whole, arrived, _, _ = stages[stage]
        return pltpu.make_async_remote_copy(
            src_ref=whole.at[pl.ds(pl.multiple_of(other * HALF, HALF), HALF)],
            dst_ref=arrived,
            send_sem=half_send.at[stage],
            recv_sem=half_recv.at[stage],
            device_id=(g, j, other),
            device_id_type=MESH,
        )

    def z_copy(stage, i):
        _, _, summed, landing = stages[stage]
        return pltpu.make_async_remote_copy(
            src_ref=summed.at[i],
            dst_ref=landing.at[source],
            send_sem=z_send.at[stage, i],
            recv_sem=z_recv.at[stage, source],
            device_id=(g, 2 * i + ta, half),
            device_id_type=MESH,
        )

    def away(i):
        return jnp.logical_or(2 * i + ta != j, half != ta)

    def z_start(stage):
        whole, arrived, summed, landing = stages[stage]
        half_copy(stage).wait_recv()
        own = whole[pl.ds(pl.multiple_of(ta * HALF, HALF), HALF), :]
        summed[...] = (own + arrived[...]).reshape(summed.shape)
        for ahead in range(N_ROW // 2):
            i = lax.rem(j // 2 + 2 + ahead, N_ROW // 2)
            pl.when(away(i))(z_copy(stage, i).start)

        @pl.when(jnp.logical_not(away(j // 2)))
        def _():
            landing[source] = summed[j // 2]

    def z_wait(stage):
        _, _, summed, landing = stages[stage]
        for src in range(N_ROW // 2):
            copy = pltpu.make_async_remote_copy(
                src_ref=summed.at[0],
                dst_ref=landing.at[src],
                send_sem=z_send.at[stage, 0],
                recv_sem=z_recv.at[stage, src],
                device_id=(g, j, other),
                device_id_type=MESH,
            )
            mine = jnp.logical_and(
                jnp.logical_and(half == ta, source == src), j % 2 == ta
            )
            pl.when(jnp.logical_not(mine))(copy.wait_recv)

    w = [window[t].astype(F32) * 0.125 for t in range(STEPS)]

    def accumulate_early():
        z = in_early[...].reshape(HALF, 2 * LANES)
        lanes = lax.broadcasted_iota(jnp.int32, (1, 2 * LANES), 1)
        scale = jnp.where(lanes < 2 * NM, w[0], jnp.where(lanes < 4 * NM, w[1], w[2]))
        high, low = split(z * scale)
        pieces = jnp.concatenate([high, low, high], axis=1)
        return jnp.dot(pieces, early[...], preferred_element_type=F32)

    def accumulate_late():
        high, low = split(in_late[...].reshape(HALF, LANES) * w[STEPS - 1])
        pieces = jnp.concatenate([high, low, high], axis=1)
        return jnp.dot(pieces, late[...], preferred_element_type=F32)

    for t in range(STEPS):
        for c in ORDER:
            for side, edge in ((0, 0), (1, CHUNKS - 1)):
                if c == edge:
                    pl.when(has["row", side])(row_wait(t, side).wait_recv)
                    at = 6 if side == 0 else 8 + CR
                    for f in range(NF):
                        state[t][f, 2 : 2 + CX, at : at + 2, :] = row_in[t, side, f]
            for side in range(2):
                pl.when(has["gx", side])(gx_wait(t, side, c).wait_recv)
            ta_copy(t, c).wait_recv()
            step_chunk(t, c)
            if t < STEPS - 1:
                send_chunk(t + 1, c)
            elif c == ORDER[1]:
                z_start(0)
        coefficients(t)
        if t < STEPS - 1:
            heard(1 << t)
        if t < STEPS - 2:
            announce(2 << t)
        if t == STEPS - 2:
            half_copy(0).start()
    half_copy(1).start()
    z_start(1)
    z_wait(0)
    acc[...] = accumulate_early()
    for t in range(STEPS):
        for c in range(CHUNKS):
            for side in range(2):
                pl.when(has["gx", side])(gx_copy(t, side, c).wait_send)
            ta_copy(t, c).wait_send()
        for side in range(2):
            pl.when(has["row", side])(row_copy(t, side).wait_send)
    for stage in range(2):
        half_copy(stage).wait_send()
        for i in range(N_ROW // 2):
            pl.when(away(i))(z_copy(stage, i).wait_send)
    z_wait(1)
    spectra_ref[...] = (acc[...] + accumulate_late())[:, :COLS]


def write_out(advanced_ref, spectra_ref, advanced_hbm, spectra_hbm, sem):
    copies = [
        pltpu.make_async_copy(advanced_ref, advanced_hbm, sem.at[0]),
        pltpu.make_async_copy(spectra_ref, spectra_hbm, sem.at[1]),
    ]
    for copy in copies:
        copy.start()
    for copy in copies:
        copy.wait()


def local(n_gx, conserved, diffusivity, axial_speed, coupling, weights, station_cell, owner_row, window):
    vmem = pl.BlockSpec(memory_space=pltpu.VMEM)
    hbm = pl.BlockSpec(memory_space=pltpu.HBM)
    big = pltpu.VMEM((NF, CX + 4, CR + 16, LANES), F32)
    dma = pltpu.SemaphoreType.DMA
    advanced, spectra = pl.pallas_call(
        functools.partial(kernel, n_gx),
        out_shape=(
            jax.ShapeDtypeStruct((NF, CX, CR, LANES), F32),
            jax.ShapeDtypeStruct((SLOTS // 2, COLS), F32),
        ),
        in_specs=[hbm] * 11,
        out_specs=(vmem, vmem),
        scratch_shapes=[
            big,
            big,
            big,
            big,
            pltpu.VMEM((STEPS, NF, CX, CR, LANES), F32),
            pltpu.VMEM((STEPS, 2, NF, CX, 2, LANES), F32),
            pltpu.VMEM((STEPS, 2, NF, CX, 2, LANES), F32),
            pltpu.VMEM((CX * CR, LANES), F32),
            pltpu.VMEM((SLOTS, CX * CR), BF16),
            pltpu.VMEM((STEPS, 3 * LANES, 2 * LANES), BF16),
            pltpu.VMEM((6 * LANES, WIDE), BF16),
            pltpu.VMEM((3 * LANES, WIDE), BF16),
            pltpu.VMEM((1, STN), jnp.int32),
            pltpu.VMEM((1, STN), jnp.int32),
            pltpu.SMEM((NF,), F32),
            pltpu.SMEM((NF,), F32),
            pltpu.SMEM((NF, NF), F32),
            pltpu.SMEM((NF,), F32),
            pltpu.SMEM((STEPS,), jnp.int32),
            pltpu.VMEM((SLOTS, 2 * LANES), F32),
            pltpu.VMEM((SLOTS, LANES), F32),
            pltpu.VMEM((HALF, 2 * LANES), F32),
            pltpu.VMEM((HALF, LANES), F32),
            pltpu.VMEM((N_ROW // 2, CAP, 2 * LANES), F32),
            pltpu.VMEM((N_ROW // 2, CAP, LANES), F32),
            pltpu.VMEM((N_ROW // 2, CAP, 2 * LANES), F32),
            pltpu.VMEM((N_ROW // 2, CAP, LANES), F32),
            pltpu.VMEM((HALF, WIDE), F32),
            pltpu.SemaphoreType.REGULAR((3,)),
            dma((11,)),
            dma((STEPS, 2, CHUNKS)),
            dma((STEPS, 2, CHUNKS)),
            dma((STEPS, CHUNKS)),
            dma((STEPS, CHUNKS)),
            dma((STEPS, 2)),
            dma((STEPS, 2)),
            dma((2,)),
            dma((2,)),
            dma((2, N_ROW // 2)),
            dma((2, N_ROW // 2)),
        ],
        compiler_params=pltpu.CompilerParams(
            collective_id=0, has_side_effects=True, vmem_limit_bytes=40 * 1024 * 1024
        ),
    )(
        *(
            pltpu.with_memory_space_constraint(operand, pltpu.HBM)
            for operand in (
                conserved,
                diffusivity,
                axial_speed,
                coupling,
                weights,
                window,
                station_cell.reshape(1, STN),
                owner_row.reshape(1, STN),
                jnp.asarray(azimuth_tables()),
                *(jnp.asarray(table) for table in phase_tables()),
            )
        )
    )
    advanced, spectra = pl.pallas_call(
        write_out,
        out_shape=(
            jax.ShapeDtypeStruct(advanced.shape, F32),
            jax.ShapeDtypeStruct(spectra.shape, F32),
        ),
        in_specs=[pl.BlockSpec(memory_space=pl.ANY)] * 2,
        out_specs=(hbm, hbm),
        compiler_params=pltpu.CompilerParams(vmem_limit_bytes=1024 * 1024),
        scratch_shapes=[dma((2,))],
    )(advanced, spectra)
    return advanced, spectra[None]


def solution(mesh):
    in_specs = (
        P(None, "gx", "row", "ta"),
        P(),
        P(),
        P(),
        P(),
        P(("gx", "row")),
        P(("gx", "row"), None),
        P(),
    )
    out_specs = (P(None, "gx", "row", "ta"), P(("gx", "row"), "ta", None))
    return jax.shard_map(
        functools.partial(local, mesh.shape["gx"]),
        mesh=mesh,
        in_specs=in_specs,
        out_specs=out_specs,
        check_vma=False,
    )
```

```python
import functools
import math

import jax
import jax.numpy as jnp
import numpy as np
from jax import lax
from jax.experimental import pallas as pl
from jax.experimental.pallas import tpu as pltpu
from jax.sharding import PartitionSpec as P

NF = 5
CX = 8
CR = 32
LANES = 128
NTH = 256
NM = 33
NFREQ = 16
STEPS = 4
CAP = 16
STN = 32
N_ROW = 8
SLOTS = N_ROW * CAP
HALF = SLOTS // 2
COLS = NFREQ * 2 * NM
WIDE = 1152
MESH = pl.DeviceIdType.MESH
F32 = jnp.float32
BF16 = jnp.bfloat16
ORDER = (0, 3, 1, 2)
CHUNKS = 4


def split(value):
    high = value.astype(BF16)
    return high, (value - high.astype(F32)).astype(BF16)


def in_pieces(table, axis):
    high = table.astype(jnp.bfloat16)
    low = (table - high.astype(np.float32)).astype(jnp.bfloat16)
    return np.concatenate([high, high, low], axis=axis)


def lane_of(t, part, m):
    return (0 if t == STEPS - 1 else 2 * NM * t) + NM * part + m


def azimuth_tables():
    theta = np.arange(NTH)
    turns = theta[:, None] * np.arange(NM)[None, :] % NTH
    angle = 2.0 * math.pi / NTH * turns
    table = np.zeros((STEPS, NTH, 2 * LANES), np.float32)
    for t in range(STEPS):
        table[t, :, lane_of(t, 0, 0) : lane_of(t, 0, NM)] = np.cos(angle) / math.sqrt(NTH)
        table[t, :, lane_of(t, 1, 0) : lane_of(t, 1, NM)] = np.sin(angle) / math.sqrt(NTH)
    table = table.reshape(STEPS, 2, LANES, 2 * LANES).swapaxes(0, 1)
    return in_pieces(table, 2)


def phase_tables():
    early = np.zeros((2 * LANES, WIDE), np.float32)
    late = np.zeros((LANES, WIDE), np.float32)
    for t in range(STEPS):
        rows = late if t == STEPS - 1 else early
        for k in range(NFREQ):
            phase = math.pi * (k + 1) * t / NFREQ
            for m in range(NM):
                first, second = (k * 2) * NM + m, (k * 2 + 1) * NM + m
                rows[lane_of(t, 0, m), first] = math.cos(phase)
                rows[lane_of(t, 1, m), first] = -math.sin(phase)
                rows[lane_of(t, 0, m), second] = -math.sin(phase)
                rows[lane_of(t, 1, m), second] = -math.cos(phase)
    return in_pieces(early, 0), in_pieces(late, 0)


def kernel(
    n_gx,
    x_ref,
    diffusivity_hbm,
    axial_speed_hbm,
    coupling_hbm,
    weights_hbm,
    window_hbm,
    cell_hbm,
    owner_hbm,
    table_hbm,
    early_hbm,
    late_hbm,
    out_ref,
    spectra_ref,
    s0,
    s1,
    s2,
    s3,
    mirror,
    row_out,
    row_in,
    pressure,
    place,
    table,
    early,
    late,
    cell_ref,
    owner_ref,
    diffusivity,
    axial_speed,
    coupling,
    weights,
    window,
    z_early,
    z_late,
    half_early,
    half_late,
    sum_early,
    sum_late,
    in_early,
    in_late,
    acc,
    ready,
    local_sem,
    gx_send,
    gx_recv,
    ta_send,
    ta_recv,
    row_send,
    row_recv,
    half_send,
    half_recv,
    z_send,
    z_recv,
):
    g, j, ta = lax.axis_index("gx"), lax.axis_index("row"), lax.axis_index("ta")
    other = 1 - ta
    state = (s0, s1, s2, s3)
    has = {("gx", 0): g > 0, ("gx", 1): g < n_gx - 1, ("row", 0): j > 0, ("row", 1): j < N_ROW - 1}
    to = {
        ("gx", 0): (g - 1, j, ta),
        ("gx", 1): (g + 1, j, ta),
        ("row", 0): (g, j - 1, ta),
        ("row", 1): (g, j + 1, ta),
    }

    loads = [
        pltpu.make_async_copy(x_ref, s0.at[:, 2 : 2 + CX, 8 : 8 + CR, :], local_sem.at[0]),
        pltpu.make_async_copy(table_hbm.at[ta], table, local_sem.at[1]),
        pltpu.make_async_copy(early_hbm, early, local_sem.at[2]),
        pltpu.make_async_copy(late_hbm, late, local_sem.at[3]),
        pltpu.make_async_copy(cell_hbm, cell_ref, local_sem.at[4]),
        pltpu.make_async_copy(owner_hbm, owner_ref, local_sem.at[5]),
        pltpu.make_async_copy(diffusivity_hbm, diffusivity, local_sem.at[6]),
        pltpu.make_async_copy(axial_speed_hbm, axial_speed, local_sem.at[7]),
        pltpu.make_async_copy(coupling_hbm, coupling, local_sem.at[8]),
        pltpu.make_async_copy(weights_hbm, weights, local_sem.at[9]),
        pltpu.make_async_copy(window_hbm, window, local_sem.at[10]),
    ]
    for load in loads:
        load.start()

    barrier = pltpu.get_barrier_semaphore()
    sides = (("gx", 0), ("gx", 1), ("row", 0), ("row", 1))
    for key in sides:

        @pl.when(has[key])
        def _():
            pl.semaphore_signal(barrier, 1, device_id=to[key], device_id_type=MESH)

    pl.semaphore_signal(barrier, 1, device_id=(g, j, other), device_id_type=MESH)

    def in_range(distance):
        return (j - distance >= 0, j - distance), (j + distance < N_ROW, j + distance)

    def announce(distance):
        for inside, owner in in_range(distance):

            @pl.when(inside)
            def _():
                pl.semaphore_signal(
                    ready.at[distance // 2], 1, device_id=(g, owner, ta), device_id_type=MESH
                )

        if distance == 1:
            pl.semaphore_signal(ready.at[0], 1, device_id=(g, j, other), device_id_type=MESH)

    def heard(distance):
        count = 1 if distance == 1 else 0
        for inside, _ in in_range(distance):
            count = count + jnp.where(inside, 1, 0)
        pl.semaphore_wait(ready.at[distance // 2], count)

    for side in range(2):

        @pl.when(jnp.logical_not(has["gx", side]))
        def _():
            for s in state:
                s[:, 10 * side : 10 * side + 2, 8 : 8 + CR, :] = jnp.zeros((NF, 2, CR, LANES), F32)

        @pl.when(jnp.logical_not(has["row", side]))
        def _():
            for t in range(STEPS):
                row_in[t, side] = jnp.zeros((NF, CX, 2, LANES), F32)


    def gx_copy(t, side, c):
        rows = pl.ds(8 + 8 * c, 8)
        return pltpu.make_async_remote_copy(
            src_ref=state[t].at[:, pl.ds(8 * side - 2 * side + 2, 2), rows, :],
            dst_ref=state[t].at[:, pl.ds(10 - 10 * side, 2), rows, :],
            send_sem=gx_send.at[t, side, c],
            recv_sem=gx_recv.at[t, 1 - side, c],
            device_id=to["gx", side],
            device_id_type=MESH,
        )

    def gx_wait(t, side, c):
        rows = pl.ds(8 + 8 * c, 8)
        return pltpu.make_async_remote_copy(
            src_ref=state[t].at[:, pl.ds(2, 2), rows, :],
            dst_ref=state[t].at[:, pl.ds(10 * side, 2), rows, :],
            send_sem=gx_send.at[t, side, c],
            recv_sem=gx_recv.at[t, side, c],
            device_id=to["gx", side],
            device_id_type=MESH,
        )

    def row_copy(t, side):
        return pltpu.make_async_remote_copy(
            src_ref=x_ref.at[:, :, pl.ds((CR - 2) * side, 2), :] if t == 0 else row_out.at[t, side],
            dst_ref=row_in.at[t, 1 - side],
            send_sem=row_send.at[t, side],
            recv_sem=row_recv.at[t, 1 - side],
            device_id=to["row", side],
            device_id_type=MESH,
        )

    def row_wait(t, side):
        return pltpu.make_async_remote_copy(
            src_ref=row_out.at[t, side],
            dst_ref=row_in.at[t, side],
            send_sem=row_send.at[t, side],
            recv_sem=row_recv.at[t, side],
            device_id=to["row", side],
            device_id_type=MESH,
        )

    def ta_copy(t, c):
        return pltpu.make_async_remote_copy(
            src_ref=state[t].at[:, 2 : 2 + CX, pl.ds(8 + 8 * c, 8), :],
            dst_ref=mirror.at[t, :, :, pl.ds(8 * c, 8), :],
            send_sem=ta_send.at[t, c],
            recv_sem=ta_recv.at[t, c],
            device_id=(g, j, other),
            device_id_type=MESH,
        )

    def send_chunk(t, c):
        for side, edge in ((0, 0), (1, CHUNKS - 1)):
            if c == edge and t > 0:
                pl.when(has["row", side])(row_copy(t, side).start)
        for side in range(2):
            pl.when(has["gx", side])(gx_copy(t, side, c).start)
        ta_copy(t, c).start()

    peers = 1
    for key in sides:
        peers = peers + jnp.where(has[key], 1, 0)
    pl.semaphore_wait(barrier, peers)
    for side in range(2):
        pl.when(has["row", side])(row_copy(0, side).start)
    loads[0].wait()
    for c in ORDER:
        send_chunk(0, c)
    announce(1)

    for load in loads[1:]:
        load.wait()

    eye = lax.broadcasted_iota(jnp.int32, (STN, STN), 0) == lax.broadcasted_iota(jnp.int32, (STN, STN), 1)
    before = lax.broadcasted_iota(jnp.int32, (STN, STN), 0) < lax.broadcasted_iota(jnp.int32, (STN, STN), 1)
    owners = owner_ref[...]
    owner_across = jnp.broadcast_to(owners, (STN, STN)).astype(F32)
    owner_down = jnp.sum(jnp.where(eye, owner_across, 0.0), axis=1, keepdims=True)
    same = jnp.logical_and(before, owner_down == owner_across)
    rank = jnp.sum(jnp.where(same, 1.0, 0.0), axis=0, keepdims=True)
    slot = ((owners % 2) * HALF + (owners // 2) * CAP).astype(F32) + rank
    slots = lax.broadcasted_iota(jnp.int32, (SLOTS, STN), 0).astype(F32)
    slot_onehot = jnp.where(slots == slot, 1.0, 0.0).astype(BF16)
    station = cell_ref[...]
    local_cell = (station // (CR * N_ROW) - g * CX) * CR + (station % (CR * N_ROW) - j * CR)
    cell_across = jnp.broadcast_to(local_cell, (STN, STN)).astype(F32)
    cell_down = jnp.sum(jnp.where(eye, cell_across, 0.0), axis=1, keepdims=True)
    cells = lax.broadcasted_iota(jnp.int32, (STN, CX * CR), 1).astype(F32)
    cell_onehot = jnp.where(cells == cell_down, 1.0, 0.0).astype(BF16)
    place[...] = jnp.dot(slot_onehot, cell_onehot, preferred_element_type=F32).astype(BF16)

    lane = lax.broadcasted_iota(jnp.int32, (8, LANES), 1)
    first1, first2 = lane < 1, lane < 2
    last1, last2 = lane >= LANES - 1, lane >= LANES - 2
    rate = [diffusivity[f] * (1.0 / 12.0) for f in range(NF)]
    velocity = [axial_speed[f] * (1.0 / 12.0) for f in range(NF)]
    mix = [
        [coupling[f, h] + (1.0 - 7.5 * diffusivity[f] if f == h else 0.0) for h in range(NF)]
        for f in range(NF)
    ]
    press = [weights[f] for f in range(NF)]

    def step_chunk(t, c):
        s = state[t]
        r0 = 8 + 8 * c

        def body(x, carry):
            center = [s[f, x + 2, r0 : r0 + 8, :] for f in range(NF)]
            total = None
            for f in range(NF):
                v = center[f]
                o = mirror[t, f, x, 8 * c : 8 * c + 8, :]
                up1, up2 = s[f, x + 3, r0 : r0 + 8, :], s[f, x + 4, r0 : r0 + 8, :]
                dn1, dn2 = s[f, x + 1, r0 : r0 + 8, :], s[f, x, r0 : r0 + 8, :]
                near = (up1 + dn1) + (s[f, x + 2, r0 + 1 : r0 + 9, :] + s[f, x + 2, r0 - 1 : r0 + 7, :])
                far = (up2 + dn2) + (s[f, x + 2, r0 + 2 : r0 + 10, :] + s[f, x + 2, r0 - 2 : r0 + 6, :])
                near = near + (
                    pltpu.roll(jnp.where(first1, o, v), LANES - 1, 1)
                    + pltpu.roll(jnp.where(last1, o, v), 1, 1)
                )
                far = far + (
                    pltpu.roll(jnp.where(first2, o, v), LANES - 2, 1)
                    + pltpu.roll(jnp.where(last2, o, v), 2, 1)
                )
                gradient = 8.0 * (up1 - dn1) - (up2 - dn2)
                new = rate[f] * (16.0 * near - far) - velocity[f] * gradient
                for h in range(NF):
                    new = new + mix[f][h] * center[h]
                if t < STEPS - 1:
                    state[t + 1][f, x + 2, r0 : r0 + 8, :] = new
                    if c == 0:
                        row_out[t + 1, 0, f, x] = new[0:2]
                    if c == CHUNKS - 1:
                        row_out[t + 1, 1, f, x] = new[6:8]
                else:
                    out_ref[f, x, 8 * c : 8 * c + 8, :] = new
                part = press[f] * new
                total = part if total is None else total + part
            pressure[pl.ds(x * CR + 8 * c, 8), :] = total
            return carry

        lax.fori_loop(0, CX, body, 0, unroll=True)

    def coefficients(t):
        high, low = split(pressure[...])
        both = jnp.dot(place[...], jnp.concatenate([high, low], axis=1), preferred_element_type=F32)
        high, low = split(both[:, :LANES] + both[:, LANES:])
        pieces = jnp.concatenate([high, low, high], axis=1)
        if t == STEPS - 1:
            z_late[...] = jnp.dot(pieces, table[t, :, :LANES], preferred_element_type=F32)
        else:
            new = jnp.dot(pieces, table[t], preferred_element_type=F32)
            z_early[...] = new if t == 0 else z_early[...] + new

    half = j // (N_ROW // 2)
    source = j % (N_ROW // 2)
    stages = ((z_early, half_early, sum_early, in_early), (z_late, half_late, sum_late, in_late))

    def half_copy(stage):
        whole, arrived, _, _ = stages[stage]
        return pltpu.make_async_remote_copy(
            src_ref=whole.at[pl.ds(pl.multiple_of(other * HALF, HALF), HALF)],
            dst_ref=arrived,
            send_sem=half_send.at[stage],
            recv_sem=half_recv.at[stage],
            device_id=(g, j, other),
            device_id_type=MESH,
        )

    def z_copy(stage, i):
        _, _, summed, landing = stages[stage]
        return pltpu.make_async_remote_copy(
            src_ref=summed.at[i],
            dst_ref=landing.at[source],
            send_sem=z_send.at[stage, i],
            recv_sem=z_recv.at[stage, source],
            device_id=(g, 2 * i + ta, half),
            device_id_type=MESH,
        )

    def away(i):
        return jnp.logical_or(2 * i + ta != j, half != ta)

    def z_start(stage):
        whole, arrived, summed, landing = stages[stage]
        half_copy(stage).wait_recv()
        own = whole[pl.ds(pl.multiple_of(ta * HALF, HALF), HALF), :]
        summed[...] = (own + arrived[...]).reshape(summed.shape)
        for ahead in range(N_ROW // 2):
            i = lax.rem(j // 2 + 2 + ahead, N_ROW // 2)
            pl.when(away(i))(z_copy(stage, i).start)

        @pl.when(jnp.logical_not(away(j // 2)))
        def _():
            landing[source] = summed[j // 2]

    def z_wait(stage):
        _, _, summed, landing = stages[stage]
        for src in range(N_ROW // 2):
            copy = pltpu.make_async_remote_copy(
                src_ref=summed.at[0],
                dst_ref=landing.at[src],
                send_sem=z_send.at[stage, 0],
                recv_sem=z_recv.at[stage, src],
                device_id=(g, j, other),
                device_id_type=MESH,
            )
            mine = jnp.logical_and(
                jnp.logical_and(half == ta, source == src), j % 2 == ta
            )
            pl.when(jnp.logical_not(mine))(copy.wait_recv)

    w = [window[t].astype(F32) * 0.125 for t in range(STEPS)]

    def accumulate_early():
        z = in_early[...].reshape(HALF, 2 * LANES)
        lanes = lax.broadcasted_iota(jnp.int32, (1, 2 * LANES), 1)
        scale = jnp.where(lanes < 2 * NM, w[0], jnp.where(lanes < 4 * NM, w[1], w[2]))
        high, low = split(z * scale)
        pieces = jnp.concatenate([high, low, high], axis=1)
        return jnp.dot(pieces, early[...], preferred_element_type=F32)

    def accumulate_late():
        high, low = split(in_late[...].reshape(HALF, LANES) * w[STEPS - 1])
        pieces = jnp.concatenate([high, low, high], axis=1)
        return jnp.dot(pieces, late[...], preferred_element_type=F32)

    for t in range(STEPS):
        for c in ORDER:
            for side, edge in ((0, 0), (1, CHUNKS - 1)):
                if c == edge:
                    pl.when(has["row", side])(row_wait(t, side).wait_recv)
                    at = 6 if side == 0 else 8 + CR
                    for f in range(NF):
                        state[t][f, 2 : 2 + CX, at : at + 2, :] = row_in[t, side, f]
            for side in range(2):
                pl.when(has["gx", side])(gx_wait(t, side, c).wait_recv)
            ta_copy(t, c).wait_recv()
            step_chunk(t, c)
            if t < STEPS - 1:
                send_chunk(t + 1, c)
        coefficients(t)
        if t < STEPS - 1:
            heard(1 << t)
        if t < STEPS - 2:
            announce(2 << t)
        if t == STEPS - 2:
            half_copy(0).start()
            z_start(0)
    half_copy(1).start()
    z_start(1)
    z_wait(0)
    acc[...] = accumulate_early()
    for t in range(STEPS):
        for c in range(CHUNKS):
            for side in range(2):
                pl.when(has["gx", side])(gx_copy(t, side, c).wait_send)
            ta_copy(t, c).wait_send()
        for side in range(2):
            pl.when(has["row", side])(row_copy(t, side).wait_send)
    for stage in range(2):
        half_copy(stage).wait_send()
        for i in range(N_ROW // 2):
            pl.when(away(i))(z_copy(stage, i).wait_send)
    z_wait(1)
    spectra_ref[...] = (acc[...] + accumulate_late())[:, :COLS]


def write_out(advanced_ref, spectra_ref, advanced_hbm, spectra_hbm, sem):
    copies = [
        pltpu.make_async_copy(advanced_ref, advanced_hbm, sem.at[0]),
        pltpu.make_async_copy(spectra_ref, spectra_hbm, sem.at[1]),
    ]
    for copy in copies:
        copy.start()
    for copy in copies:
        copy.wait()


def local(n_gx, conserved, diffusivity, axial_speed, coupling, weights, station_cell, owner_row, window):
    vmem = pl.BlockSpec(memory_space=pltpu.VMEM)
    hbm = pl.BlockSpec(memory_space=pltpu.HBM)
    big = pltpu.VMEM((NF, CX + 4, CR + 16, LANES), F32)
    dma = pltpu.SemaphoreType.DMA
    advanced, spectra = pl.pallas_call(
        functools.partial(kernel, n_gx),
        out_shape=(
            jax.ShapeDtypeStruct((NF, CX, CR, LANES), F32),
            jax.ShapeDtypeStruct((SLOTS // 2, COLS), F32),
        ),
        in_specs=[hbm] * 11,
        out_specs=(vmem, vmem),
        scratch_shapes=[
            big,
            big,
            big,
            big,
            pltpu.VMEM((STEPS, NF, CX, CR, LANES), F32),
            pltpu.VMEM((STEPS, 2, NF, CX, 2, LANES), F32),
            pltpu.VMEM((STEPS, 2, NF, CX, 2, LANES), F32),
            pltpu.VMEM((CX * CR, LANES), F32),
            pltpu.VMEM((SLOTS, CX * CR), BF16),
            pltpu.VMEM((STEPS, 3 * LANES, 2 * LANES), BF16),
            pltpu.VMEM((6 * LANES, WIDE), BF16),
            pltpu.VMEM((3 * LANES, WIDE), BF16),
            pltpu.VMEM((1, STN), jnp.int32),
            pltpu.VMEM((1, STN), jnp.int32),
            pltpu.SMEM((NF,), F32),
            pltpu.SMEM((NF,), F32),
            pltpu.SMEM((NF, NF), F32),
            pltpu.SMEM((NF,), F32),
            pltpu.SMEM((STEPS,), jnp.int32),
            pltpu.VMEM((SLOTS, 2 * LANES), F32),
            pltpu.VMEM((SLOTS, LANES), F32),
            pltpu.VMEM((HALF, 2 * LANES), F32),
            pltpu.VMEM((HALF, LANES), F32),
            pltpu.VMEM((N_ROW // 2, CAP, 2 * LANES), F32),
            pltpu.VMEM((N_ROW // 2, CAP, LANES), F32),
            pltpu.VMEM((N_ROW // 2, CAP, 2 * LANES), F32),
            pltpu.VMEM((N_ROW // 2, CAP, LANES), F32),
            pltpu.VMEM((HALF, WIDE), F32),
            pltpu.SemaphoreType.REGULAR((3,)),
            dma((11,)),
            dma((STEPS, 2, CHUNKS)),
            dma((STEPS, 2, CHUNKS)),
            dma((STEPS, CHUNKS)),
            dma((STEPS, CHUNKS)),
            dma((STEPS, 2)),
            dma((STEPS, 2)),
            dma((2,)),
            dma((2,)),
            dma((2, N_ROW // 2)),
            dma((2, N_ROW // 2)),
        ],
        compiler_params=pltpu.CompilerParams(
            collective_id=0, has_side_effects=True, vmem_limit_bytes=40 * 1024 * 1024
        ),
    )(
        *(
            pltpu.with_memory_space_constraint(operand, pltpu.HBM)
            for operand in (
                conserved,
                diffusivity,
                axial_speed,
                coupling,
                weights,
                window,
                station_cell.reshape(1, STN),
                owner_row.reshape(1, STN),
                jnp.asarray(azimuth_tables()),
                *(jnp.asarray(table) for table in phase_tables()),
            )
        )
    )
    advanced, spectra = pl.pallas_call(
        write_out,
        out_shape=(
            jax.ShapeDtypeStruct(advanced.shape, F32),
            jax.ShapeDtypeStruct(spectra.shape, F32),
        ),
        in_specs=[pl.BlockSpec(memory_space=pl.ANY)] * 2,
        out_specs=(hbm, hbm),
        compiler_params=pltpu.CompilerParams(vmem_limit_bytes=1024 * 1024),
        scratch_shapes=[dma((2,))],
    )(advanced, spectra)
    return advanced, spectra[None]


def solution(mesh):
    in_specs = (
        P(None, "gx", "row", "ta"),
        P(),
        P(),
        P(),
        P(),
        P(("gx", "row")),
        P(("gx", "row"), None),
        P(),
    )
    out_specs = (P(None, "gx", "row", "ta"), P(("gx", "row"), "ta", None))
    return jax.shard_map(
        functools.partial(local, mesh.shape["gx"]),
        mesh=mesh,
        in_specs=in_specs,
        out_specs=out_specs,
        check_vma=False,
    )
```
